256 devices in a mesh: row: 16 (over z, y_lo), col: 16 (over x, y_hi, core).
Axes of the slice: x: 4, y: 4 (y_hi: 2, y_lo: 2; y = y_hi * 2 + y_lo), z: 8, core: 2. Of those that a mesh axis runs over, the one named last changes fastest.
Arguments:
- grad: bfloat16 [8192, 4096], P('row', 'col'), may hold values from -6 to 6
- left_basis: bfloat16 [8192, 8192], P('col', 'row'), may hold values from -0.0625 to 0.0625
- right_basis: bfloat16 [4096, 4096], P('row', 'col'), may hold values from -0.09375 to 0.09375
- exp_avg: float32 [8192, 4096], P('row', 'col'), may hold values from -4 to 4
- exp_avg_sq: float32 [8192, 4096], P('row', 'col'), may hold values from 0.05 to 2
Outputs:
- update: float32 [8192, 4096], P('row', 'col')
- new_avg: float32 [8192, 4096], P('row', 'col')
- new_sq: float32 [8192, 4096], P('row', 'col')
The draws below stay inside these ranges and needn't reach their ends.
All inputs are finite; a program needn't handle non-finite values.
Results may differ from the reference program's by a relative error of at most 0.0041.
Values may be sent and summed in bfloat16 or wider, within the bound.
A program may use at most 64 MiB of HBM per device.

```python
import math
import jax
import jax.numpy as jnp

M = 8192
STEP = 10
N = 4096


def level_of(rng, dims, pieces, smallest, high):
    gain, own = 1.0, jax.random.fold_in(rng, 6)
    for dim, parts in pieces:
        heights = jnp.exp(jax.random.uniform(jax.random.fold_in(own, dim), (parts,), jnp.float32, smallest / len(pieces), high / len(pieces)))
        gain = gain * jnp.repeat(heights, dims[dim] // parts).reshape([-1 if axis == dim else 1 for axis in range(len(dims))])
    return gain


def centred(own_key, extent, deviation, limit, pieces=(), held_as=jnp.bfloat16):
    entries = deviation * jax.random.normal(own_key, extent, jnp.float32)
    if pieces:
        entries = entries * level_of(own_key, extent, pieces, -0.22, 0.18)
    return jnp.clip(entries, -limit, limit).astype(held_as)


def setup_inputs(seed: int = 0) -> dict:
    keys = jax.random.split(jax.random.key(seed), 6)
    return {
        "grad": centred(keys[0], (M, N), 1.0, 6.0, ((0, 16), (1, 16))),
        "left_basis": centred(keys[1], (M, M), M ** -0.5, 0.0625, ((0, 16), (1, 16))),
        "right_basis": centred(keys[2], (N, N), N ** -0.5, 0.09375, ((0, 16), (1, 16))),
        "exp_avg": centred(keys[3], (M, N), 0.5, 4.0, ((0, 16), (1, 16)), jnp.float32),
        "exp_avg_sq": jnp.clip(jnp.exp(math.log(2.0) - 3.6888794 * jax.random.uniform(keys[4], (M, N), jnp.float32) ** level_of(keys[4], (M, N), ((0, 16), (1, 16)), -0.2, 0.2)), 0.05, 2.0),
    }


beta_first = 0.95
beta_second = 0.95
epsilon = 1e-08

def reference(grad, left_basis, right_basis, exp_avg, exp_avg_sq):
    rotated = jnp.dot(left_basis.T, grad, preferred_element_type=jnp.float32).astype(jnp.bfloat16)
    projected = jnp.dot(rotated, right_basis, preferred_element_type=jnp.float32)
    new_avg = beta_first * exp_avg + (1.0 - beta_first) * projected
    new_sq = beta_second * exp_avg_sq + (1.0 - beta_second) * projected * projected
    first_fix = 1.0 - beta_first ** STEP
    second_fix = 1.0 - beta_second ** STEP
    direction = (new_avg / first_fix / (jnp.sqrt(new_sq / second_fix) + epsilon)).astype(jnp.bfloat16)
    back = jnp.dot(left_basis, direction, preferred_element_type=jnp.float32).astype(jnp.bfloat16)
    update = jnp.dot(back, right_basis.T, preferred_element_type=jnp.float32)
    return (update, new_avg, new_sq)
```

```python
import functools

import jax
import jax.numpy as jnp
from jax import lax
from jax.experimental import pallas as pl
from jax.experimental.pallas import tpu as pltpu
from jax.sharding import PartitionSpec as P

STEP = 10
beta_first = 0.95
beta_second = 0.95
epsilon = 1e-08

MESH = pl.DeviceIdType.MESH
F32 = jnp.float32
BF16 = jnp.bfloat16

COPIES = 96


def dot(a, b, dims):
    return lax.dot_general(a, b, (dims, ((), ())), preferred_element_type=F32)


NN = ((1,), (0,))
TN = ((0,), (0,))
NT = ((1,), (1,))


def kernel(
    g_ref, l_ref, r_ref, avg_ref, sq_ref,
    update_ref, new_avg_ref, new_sq_ref,
    gbuf, lbuf, rbuf, rot, part, part_in, proj, proj_in, dbuf,
    wsend, wrecv, hilo, ssend, srecv, tsend, trecv,
    ssem, rsem, lsem,
):
    row, col = lax.axis_index("row"), lax.axis_index("col")
    z, h = row // 2, row % 2
    x, t, j = col // 4, (col // 2) % 2, col % 2
    matched = h == j
    half = 256
    lo, hi = pl.ds(0, half), pl.ds(half, half)

    def zq(d):
        return (z + d + 8) % 8

    def xq(d, other):
        return 2 * ((x + d + 4) % 4) + (1 - t if other else t)

    zp, zm = (2 * zq(1) + h, col), (2 * zq(-1) + h, col)
    xp, xm = (row, (col + 4) % 16), (row, (col + 12) % 16)
    yh = (row, 4 * x + 2 * (1 - t) + j)
    yl = (2 * z + 1 - h, col)
    core = (row, 4 * x + 2 * t + 1 - j)
    diag = (2 * z + 1 - h, 4 * x + 2 * t + 1 - j)

    barrier = pltpu.get_barrier_semaphore()
    for who in (zp, zm, xp, xm, yh, yl, core, diag):
        pl.semaphore_signal(barrier, inc=1, device_id=who, device_id_type=MESH)
    pl.semaphore_wait(barrier, 8)

    count = [0]
    sent = []

    def make(src, dst, who, slot=None):
        if slot is None:
            slot = count[0]
            count[0] += 1
        return pltpu.make_async_remote_copy(
            src_ref=src, dst_ref=dst, send_sem=ssem.at[slot], recv_sem=rsem.at[slot],
            device_id=who, device_id_type=MESH,
        )

    def push(src, dst, who):
        copy = make(src, dst, who)
        copy.start()
        sent.append(copy)
        return copy

    def same(ref, who):
        return push(ref, ref, who)

    own_g = pltpu.make_async_copy(g_ref, gbuf.at[z], lsem.at[0])
    own_g.start()
    swap = make(l_ref, lbuf.at[1 - j, xq(0, False)], diag)
    own_l = pltpu.make_async_copy(l_ref, lbuf.at[j, xq(0, False)], lsem.at[1])

    @pl.when(matched)
    def _():
        own_l.start()

    @pl.when(jnp.logical_not(matched))
    def _():
        swap.start()

    base_r = count[0]
    count[0] += 3
    r_far = make(r_ref, rbuf.at[z, j], (2 * z + 1 - h, 4 * x + 2 * t + h), base_r + j)
    r_near = make(r_ref, rbuf.at[z, j], core, base_r + 2)
    r_own = pltpu.make_async_copy(r_ref, rbuf.at[z, j], lsem.at[2])
    r_far.start()

    @pl.when(matched)
    def _():
        r_own.start()
        own_l.wait()

    @pl.when(jnp.logical_not(matched))
    def _():
        r_near.start()

    own_g.wait()

    class RingZ:
        def __init__(self, buf, cut):
            self.buf, self.cut = buf, cut

        def start(self):
            self.p, self.m = same(self.buf.at[z], zp), same(self.buf.at[z], zm)

        def step(self, k):
            self.p.wait_recv()
            down = self.buf.at[zq(-k)]
            self.p = same(down if k < 3 else self.cut(down, 0), zp)
            self.m.wait_recv()
            up = self.buf.at[zq(k)]
            self.m = same(up if k < 3 else self.cut(up, 1), zm)

        def finish(self):
            self.p.wait_recv()
            self.m.wait_recv()

    class RingX:
        def __init__(self, buf, share):
            self.buf, self.share = buf, share
            self.p, self.m = {}, {}

        def go(self, other):
            block = self.buf.at[xq(0, other)]
            if not other:
                self.y = same(block, yh)
            self.p[other], self.m[other] = same(block, xp), same(block, xm)
            self.share(xq(0, other))

        def second(self):
            self.y.wait_recv()
            self.go(True)

        def forward(self, other):
            self.p[other].wait_recv()
            q = xq(-1, other)
            self.p[other] = same(self.buf.at[q, lo], xp)
            self.share(q)
            self.m[other].wait_recv()
            q = xq(1, other)
            self.m[other] = same(self.buf.at[q, hi], xm)
            self.share(q)

        def finish(self, other):
            self.p[other].wait_recv()
            self.m[other].wait_recv()
            self.share(xq(2, other))

    shared = []

    def share_left(q):
        shared.append(same(lbuf.at[j, q], core))

    rows_cut = lambda ref, k: ref.at[lo if k == 0 else hi]
    ring_g = RingZ(gbuf, rows_cut)
    ring_r = RingZ(rbuf, lambda ref, k: ref.at[k])
    ring_l = RingX(lbuf.at[j], share_left)

    ring_g.start()

    @pl.when(jnp.logical_not(matched))
    def _():
        swap.wait_recv()

    ring_l.go(False)
    ring_g.step(1)

    @pl.when(matched)
    def _():
        make(r_ref, rbuf.at[z, 1 - j], core, base_r + 2).wait_recv()
        r_own.wait()

    @pl.when(jnp.logical_not(matched))
    def _():
        make(r_ref, rbuf.at[z, 0], core, base_r).wait_recv()
        make(r_ref, rbuf.at[z, 1], core, base_r + 1).wait_recv()

    ring_l.second()
    ring_g.step(2)
    ring_r.start()
    ring_l.forward(False)
    ring_g.step(3)
    ring_r.step(1)
    ring_l.forward(True)
    ring_g.finish()
    ring_r.step(2)

    part[...] = jnp.zeros_like(part)

    def rotate(q):
        for i in range(2):
            part[i] += dot(lbuf[i, q], gbuf[q], TN)

    for copy in shared[:6]:
        copy.wait_recv()

    def near(n, carry):
        q = 2 * ((x + n // 2 + 3) % 4) + n % 2
        rotate(q)
        return carry

    lax.fori_loop(0, 6, near, 0)
    ring_l.finish(False)
    ring_l.finish(True)
    for copy in shared[6:]:
        copy.wait_recv()

    def far(n, carry):
        rotate(2 * ((x + 2) % 4) + n)
        return carry

    lax.fori_loop(0, 2, far, 0)
    exchange = push(part.at[1 - h], part_in, yl)
    ring_r.step(3)
    exchange.wait_recv()
    rot[xq(0, False)] = (part[h] + part_in[...]).astype(BF16)

    ring_rot = RingX(rot, lambda q: None)
    ring_rot.go(False)
    ring_r.finish()
    ring_rot.second()
    ring_rot.forward(False)
    ring_rot.forward(True)

    proj[...] = jnp.zeros_like(proj)

    def project(q):
        for c in range(2):
            proj[c] += dot(rot[q], rbuf[q, c], NN)

    def near_p(n, carry):
        project(2 * ((x + n // 2 + 3) % 4) + n % 2)
        return carry

    lax.fori_loop(0, 6, near_p, 0)
    ring_rot.finish(False)
    ring_rot.finish(True)

    def far_p(n, carry):
        project(2 * ((x + 2) % 4) + n)
        return carry

    lax.fori_loop(0, 2, far_p, 0)
    cross = push(proj.at[1 - j], proj_in, core)
    cross.wait_recv()
    projected = proj[j] + proj_in[...]
    new_avg = beta_first * avg_ref[...] + (1.0 - beta_first) * projected
    new_sq = beta_second * sq_ref[...] + (1.0 - beta_second) * projected * projected
    new_avg_ref[...] = new_avg
    new_sq_ref[...] = new_sq
    first_fix = 1.0 - beta_first**STEP
    second_fix = 1.0 - beta_second**STEP
    dbuf[h] = (new_avg / first_fix / (jnp.sqrt(new_sq / second_fix) + epsilon)).astype(BF16)
    push(dbuf.at[h], dbuf.at[h], yl).wait_recv()

    def spread_left(q, rows):
        return dot(lbuf[0, q, rows], dbuf[0], NN) + dot(lbuf[1, q, rows], dbuf[1], NN)

    both = ((lo, 0), (hi, 1))
    flying = {}
    for s in range(1, 5):
        for way, who, first in ((0, zp, 0), (1, zm, 1)):
            q = zq(5 - s if way == 0 else s - 5)
            for rows, k in (both[1 - first], both[first]):
                if s == 1 and k != first:
                    continue
                value = spread_left(q, rows)
                before = flying.get((way, s - 1, k))
                if before is not None:
                    before.wait_recv()
                    value += wrecv[way, s - 2, rows].astype(F32)
                wsend[way, s - 1, rows] = value.astype(BF16)
                flying[way, s, k] = push(
                    wsend.at[way, s - 1, rows], wrecv.at[way, s - 1, rows], who
                )
    for rows, k in both:
        value = spread_left(z, rows)
        for way in range(2):
            flying[way, 4, k].wait_recv()
            value += wrecv[way, 3, rows].astype(F32)
        high = value.astype(BF16)
        hilo[j, 0, rows] = high
        hilo[j, 1, rows] = (value - high.astype(F32)).astype(BF16)
    push(hilo.at[j], hilo.at[j], core).wait_recv()

    def spread_right(q, rows):
        total = dot(hilo[0, 0, rows], rbuf[q, 0], NT)
        total += dot(hilo[1, 0, rows], rbuf[q, 1], NT)
        total += dot(hilo[0, 1, rows], rbuf[q, 0], NT)
        total += dot(hilo[1, 1, rows], rbuf[q, 1], NT)
        return total

    going = {}

    def send(o, way, s, rows, k, value):
        ssend[o, way, s, rows] = value.astype(BF16)
        going[o, way, s, k] = push(
            ssend.at[o, way, s, rows], srecv.at[o, way, s, rows], (xp, xm)[way]
        )

    for o in (1, 0):
        for way in range(2):
            rows, k = both[way]
            send(o, way, 0, rows, k, spread_right(xq(2, o == 1), rows))
        for way in range(2):
            rows, k = both[1 - way]
            send(o, way, 1, rows, k, spread_right(xq(1 - 2 * way, o == 1), rows))
    for o in (1, 0):
        for way in range(2):
            rows, k = both[way]
            value = spread_right(xq(1 - 2 * way, o == 1), rows)
            going[o, way, 0, k].wait_recv()
            send(o, way, 1, rows, k, value + srecv[o, way, 0, rows].astype(F32))
    last = {}
    for o in (1, 0):
        for rows, k in both:
            value = spread_right(xq(0, o == 1), rows)
            for way in range(2):
                going[o, way, 1, k].wait_recv()
                value += srecv[o, way, 1, rows].astype(F32)
            if o == 1:
                tsend[rows] = value.astype(BF16)
                last[k] = push(tsend.at[rows], trecv.at[rows], yh)
            else:
                last[k].wait_recv()
                update_ref[rows] = value + trecv[rows].astype(F32)

    for copy in sent:
        copy.wait_send()
    r_far.wait_send()

    @pl.when(jnp.logical_not(matched))
    def _():
        swap.wait_send()
        r_near.wait_send()


def shards(grad, left_basis, right_basis, exp_avg, exp_avg_sq):
    block = jax.ShapeDtypeStruct((512, 256), F32)
    vmem = pl.BlockSpec(memory_space=pltpu.VMEM)
    return pl.pallas_call(
        kernel,
        out_shape=(block, block, block),
        in_specs=[vmem] * 5,
        out_specs=(vmem,) * 3,
        scratch_shapes=[
            pltpu.VMEM((8, 512, 256), BF16),
            pltpu.VMEM((2, 8, 512, 512), BF16),
            pltpu.VMEM((8, 2, 256, 256), BF16),
            pltpu.VMEM((8, 512, 256), BF16),
            pltpu.VMEM((2, 512, 256), F32),
            pltpu.VMEM((512, 256), F32),
            pltpu.VMEM((2, 512, 256), F32),
            pltpu.VMEM((512, 256), F32),
            pltpu.VMEM((2, 512, 256), BF16),
            pltpu.VMEM((2, 4, 512, 256), BF16),
            pltpu.VMEM((2, 4, 512, 256), BF16),
            pltpu.VMEM((2, 2, 512, 256), BF16),
            pltpu.VMEM((2, 2, 2, 512, 256), BF16),
            pltpu.VMEM((2, 2, 2, 512, 256), BF16),
            pltpu.VMEM((512, 256), BF16),
            pltpu.VMEM((512, 256), BF16),
            pltpu.SemaphoreType.DMA((COPIES,)),
            pltpu.SemaphoreType.DMA((COPIES,)),
            pltpu.SemaphoreType.DMA((3,)),
        ],
        compiler_params=pltpu.CompilerParams(
            collective_id=0, has_side_effects=True, vmem_limit_bytes=56 * 1024 * 1024
        ),
        cost_estimate=pl.CostEstimate(flops=6_500_000_000, bytes_accessed=4_000_000, transcendentals=0),
    )(grad, left_basis, right_basis, exp_avg, exp_avg_sq)


def solution(mesh):
    return jax.shard_map(
        shards,
        mesh=mesh,
        in_specs=(
            P("row", "col"),
            P("col", "row"),
            P("row", "col"),
            P("row", "col"),
            P("row", "col"),
        ),
        out_specs=(P("row", "col"), P("row", "col"), P("row", "col")),
        check_vma=False,
    )
```

```python
import functools

import jax
import jax.numpy as jnp
from jax import lax
from jax.experimental import pallas as pl
from jax.experimental.pallas import tpu as pltpu
from jax.sharding import PartitionSpec as P

STEP = 10
beta_first = 0.95
beta_second = 0.95
epsilon = 1e-08

MESH = pl.DeviceIdType.MESH
F32 = jnp.float32
BF16 = jnp.bfloat16

COPIES = 160


def dot(a, b, dims):
    return lax.dot_general(a, b, (dims, ((), ())), preferred_element_type=F32)


NN = ((1,), (0,))
TN = ((0,), (0,))
NT = ((1,), (1,))


def kernel(
    g_ref, l_ref, r_ref, avg_in, sq_in,
    update_out, avg_out, sq_out,
    update, avg, sq,
    gbuf, lbuf, rbuf, rot, part, part_in, proj, proj_in, dbuf,
    whole, wsend, wrecv, hilo, ssend, srecv, keep, tsend, trecv,
    ssem, rsem, lsem,
):
    row, col = lax.axis_index("row"), lax.axis_index("col")
    z, h = row // 2, row % 2
    x, t, j = col // 4, (col // 2) % 2, col % 2
    matched = h == j
    half = 256
    lo, hi = pl.ds(0, half), pl.ds(half, half)

    def zq(d):
        return (z + d + 8) % 8

    def xq(d, other):
        return 2 * ((x + d + 4) % 4) + (1 - t if other else t)

    zp, zm = (2 * zq(1) + h, col), (2 * zq(-1) + h, col)
    xp, xm = (row, (col + 4) % 16), (row, (col + 12) % 16)
    yh = (row, 4 * x + 2 * (1 - t) + j)
    yl = (2 * z + 1 - h, col)
    core = (row, 4 * x + 2 * t + 1 - j)
    diag = (2 * z + 1 - h, 4 * x + 2 * t + 1 - j)

    count = [0]
    sent = []

    def make(src, dst, who, slot=None):
        if slot is None:
            slot = count[0]
            count[0] += 1
        return pltpu.make_async_remote_copy(
            src_ref=src, dst_ref=dst, send_sem=ssem.at[slot], recv_sem=rsem.at[slot],
            device_id=who, device_id_type=MESH,
        )

    def push(src, dst, who):
        copy = make(src, dst, who)
        copy.start()
        sent.append(copy)
        return copy

    def later(src, dst, who):
        copy = make(src, dst, who)
        sent.append(copy)
        return copy

    def same(ref, who):
        return push(ref, ref, who)

    halves = ((0, 256), (256, 256))

    first = xq(0, False)
    own_g = pltpu.make_async_copy(g_ref, gbuf.at[z], lsem.at[0])
    own_l = pltpu.make_async_copy(l_ref, lbuf.at[j, first], lsem.at[1])
    r_own = pltpu.make_async_copy(r_ref, rbuf.at[z, j], lsem.at[2])
    swaps = [
        make(l_ref.at[pl.ds(*r)], lbuf.at[1 - j, first, pl.ds(*r)], diag) for r in halves
    ]

    keep_avg = pltpu.make_async_copy(avg_in, avg, lsem.at[3])
    keep_sq = pltpu.make_async_copy(sq_in, sq, lsem.at[4])
    own_g.start()
    keep_avg.start()
    keep_sq.start()

    @pl.when(matched)
    def _():
        own_l.start()
        r_own.start()

    barrier = pltpu.get_barrier_semaphore()
    for who in (zp, zm, xp, xm, yh, yl, core, diag):
        pl.semaphore_signal(barrier, inc=1, device_id=who, device_id_type=MESH)
    pl.semaphore_wait(barrier, 8)

    @pl.when(jnp.logical_not(matched))
    def _():
        for copy in swaps:
            copy.start()

    base_r = count[0]
    count[0] += 3
    r_far = make(r_ref, rbuf.at[z, j], (2 * z + 1 - h, 4 * x + 2 * t + h), base_r + j)
    r_near = make(r_ref, rbuf.at[z, j], core, base_r + 2)

    def drain():
        for copy in sent:
            copy.wait_send()
        r_far.wait_send()

        @pl.when(jnp.logical_not(matched))
        def _():
            for copy in swaps:
                copy.wait_send()
            r_near.wait_send()

    class RingZ:
        def __init__(self, buf, cut):
            def both(k, low, high):
                return later(low, low, zp), later(high, high, zm)

            self.steps = [both(0, buf.at[z], buf.at[z])]
            for k in (1, 2, 3):
                low, high = buf.at[zq(-k)], buf.at[zq(k)]
                if k == 3:
                    low, high = cut(low, 0), cut(high, 1)
                self.steps.append(both(k, low, high))

        def start(self):
            for copy in self.steps[0]:
                copy.start()

        def step(self, k):
            for before, copy in zip(self.steps[k - 1], self.steps[k]):
                before.wait_recv()
                copy.start()

        def finish(self):
            for copy in self.steps[3]:
                copy.wait_recv()

    class RingX:
        def __init__(self, buf, top, size):
            low, high = pl.ds(top, size // 2), pl.ds(top + size // 2, size // 2)

            def to(q, rows, who):
                return later(buf.at[q, rows], buf.at[q, rows], who)

            self.y = to(xq(0, False), pl.ds(top, size), yh)
            self.lead, self.rest, self.passed = {}, {}, {}
            for other in (False, True):
                q = xq(0, other)
                self.lead[other] = to(q, low, xp), to(q, high, xm)
                self.rest[other] = to(q, high, xp), to(q, low, xm)
                self.passed[other] = to(xq(-1, other), low, xp), to(xq(1, other), high, xm)

        def go(self, other):
            if not other:
                self.y.start()
            for copy in self.lead[other] + self.rest[other]:
                copy.start()

        def second(self):
            self.y.wait_recv()
            self.go(True)

        def forward(self, other):
            for before, copy in zip(self.lead[other], self.passed[other]):
                before.wait_recv()
                copy.start()

        def complete(self, other):
            for copy in self.rest[other]:
                copy.wait_recv()

        def finish(self, other):
            for copy in self.passed[other]:
                copy.wait_recv()

    ring_g = RingZ(gbuf, lambda ref, k: ref.at[lo if k == 0 else hi])
    ring_r = RingZ(rbuf, lambda ref, k: ref.at[k])
    ring_l = [RingX(lbuf.at[j], *r) for r in halves]

    order = [(0, False), (-1, False), (1, False), (2, False), (0, True), (-1, True), (1, True), (2, True)]
    shared = [later(lbuf.at[j, xq(*o)], lbuf.at[j, xq(*o)], core) for o in order]

    def share(*which):
        for n in which:
            shared[n].start()

    def take(*which):
        for n in which:
            shared[n].wait_recv()

    def left(event, *which):
        for ring in ring_l:
            getattr(ring, event)(*which)

    def rotate(i, first, number):
        def body(n, carry):
            q = 2 * ((x + n // 2 + first) % 4) + n % 2
            part[i] += dot(lbuf[i, q], gbuf[q], TN)
            return carry

        lax.fori_loop(0, number, body, 0)

    pieces = tuple((128 * n, 128) for n in range(4))
    exchange = [later(part.at[1 - h, pl.ds(*r)], part_in.at[pl.ds(*r)], yl) for r in pieces]

    def give():
        for copy in exchange:
            copy.start()

    part[...] = jnp.zeros_like(part)

    @pl.when(matched)
    def _():
        own_l.wait()
        left("go", False)
        share(0)
        r_far.start()
        own_g.wait()
        ring_g.start()
        left("forward", False)
        ring_g.step(1)
        left("complete", False)
        share(1, 2)
        ring_g.step(2)
        left("finish", False)
        share(3)
        ring_g.step(3)
        make(r_ref, rbuf.at[z, 1 - j], core, base_r + 2).wait_recv()
        r_own.wait()
        ring_r.start()
        take(0, 1, 2, 4, 5, 6)
        left("second")
        share(4)
        ring_g.finish()
        rotate(1 - h, 3, 6)
        left("forward", True)
        ring_r.step(1)
        take(3, 7)
        rotate(1 - h, 2, 2)
        give()
        left("complete", True)
        share(5, 6)
        ring_r.step(2)
        rotate(h, 3, 6)
        left("finish", True)
        share(7)
        rotate(h, 2, 2)

    @pl.when(jnp.logical_not(matched))
    def _():
        own_g.wait()
        ring_g.start()
        for ring, copy in zip(ring_l, swaps):
            copy.wait_recv()
            ring.go(False)
        share(0)
        r_far.start()
        r_near.start()
        ring_g.step(1)
        left("forward", False)
        left("second")
        share(4)
        left("complete", False)
        share(1, 2)
        ring_g.step(2)
        left("forward", True)
        left("finish", False)
        share(3)
        ring_g.step(3)
        left("complete", True)
        share(5, 6)
        make(r_ref, rbuf.at[z, 0], core, base_r).wait_recv()
        make(r_ref, rbuf.at[z, 1], core, base_r + 1).wait_recv()
        ring_r.start()
        left("finish", True)
        share(7)
        ring_g.finish()
        rotate(1 - h, 0, 8)
        give()
        ring_r.step(1)
        take(0, 1, 2, 4, 5, 6)
        rotate(h, 3, 6)
        ring_r.step(2)
        take(3, 7)
        rotate(h, 2, 2)


    ring_rot = [RingX(rot, *r) for r in halves]
    for n, r in enumerate(halves):
        exchange[2 * n].wait_recv()
        exchange[2 * n + 1].wait_recv()
        rows = pl.ds(*r)
        rot[first, rows] = (part[h, rows] + part_in[rows]).astype(BF16)
        ring_rot[n].go(False)
    ring_r.step(3)
    ring_rot[0].second()
    ring_rot[0].forward(False)
    ring_rot[1].second()
    ring_rot[0].forward(True)
    ring_rot[1].forward(False)
    ring_rot[1].forward(True)
    for other in (False, True):
        ring_rot[0].complete(other)
        ring_rot[0].finish(other)
    ring_r.finish()

    keep_avg.wait()
    keep_sq.wait()
    first_fix = 1.0 - beta_first**STEP
    second_fix = 1.0 - beta_second**STEP
    give_d = []
    for n, r in enumerate(halves):
        rows = pl.ds(*r)
        if n == 1:
            for other in (False, True):
                ring_rot[1].complete(other)
                ring_rot[1].finish(other)
        proj[:, rows] = jnp.zeros((2, 256, 256), F32)

        def project(q, carry):
            for c in range(2):
                proj[c, rows] += dot(rot[q, rows], rbuf[q, c], NN)
            return carry

        lax.fori_loop(0, 8, project, 0)
        push(proj.at[1 - j, rows], proj_in.at[rows], core).wait_recv()
        projected = proj[j, rows] + proj_in[rows]
        new_avg = beta_first * avg[rows] + (1.0 - beta_first) * projected
        new_sq = beta_second * sq[rows] + (1.0 - beta_second) * projected * projected
        avg[rows] = new_avg
        sq[rows] = new_sq
        dbuf[h, rows] = (
            new_avg / first_fix / (jnp.sqrt(new_sq / second_fix) + epsilon)
        ).astype(BF16)
        give_d.append(same(dbuf.at[h, rows], yl))
    out_avg = pltpu.make_async_copy(avg, avg_out, lsem.at[3])
    out_sq = pltpu.make_async_copy(sq, sq_out, lsem.at[4])
    out_avg.start()
    out_sq.start()
    for copy in give_d:
        copy.wait_recv()

    def quarters(n):
        return (pl.ds(256 * n, 128), pl.ds(256 * n + 128, 128))

    def spread_left(q):
        whole[q] = dot(lbuf[0, q], dbuf[0], NN) + dot(lbuf[1, q], dbuf[1], NN)

    flying = {}

    def back_send(n, s, way, k):
        rows = quarters(n)[k]
        value = whole[zq(5 - s if way == 0 else s - 5), rows]
        before = flying.get((n, way, s - 1, k))
        if before is not None:
            before.wait_recv()
            value += wrecv[way, s - 2, rows].astype(F32)
        wsend[way, s - 1, rows] = value.astype(BF16)
        flying[n, way, s, k] = push(
            wsend.at[way, s - 1, rows], wrecv.at[way, s - 1, rows], (zp, zm)[way]
        )

    def back_step(n, s):
        for k in (0, 1):
            for way in (0, 1):
                if s > 2 or k == 0:
                    back_send(n, s, way, (1 - way, way)[k] if s > 2 else way)

    def back_end(n):
        rows = pl.ds(256 * n, 256)
        value = whole[z, rows]
        for way in range(2):
            for k in range(2):
                flying[n, way, 4, k].wait_recv()
        for way in range(2):
            value += wrecv[way, 3, rows].astype(F32)
        high = value.astype(BF16)
        hilo[n, j, 0] = high
        hilo[n, j, 1] = (value - high.astype(F32)).astype(BF16)
        push(hilo.at[n, j], hilo.at[n, j], core).wait_recv()

    def spread_right(n, q):
        total = dot(hilo[n, 0].reshape(512, 256), rbuf[q, 0], NT)
        total += dot(hilo[n, 1].reshape(512, 256), rbuf[q, 1], NT)
        return total[:256] + total[256:]

    going, kept, last = {}, {}, {}

    def send(n, o, way, s, k, value):
        rows = quarters(n)[k]
        ssend[o, way, s, rows] = value.astype(BF16)
        going[n, o, way, s, k] = push(
            ssend.at[o, way, s, rows], srecv.at[o, way, s, rows], (xp, xm)[way]
        )

    def part_of(value, k):
        return value[128 * k : 128 * k + 128]

    def up_first(n):
        for o in (1, 0):
            value = spread_right(n, xq(2, o == 1))
            for way in range(2):
                send(n, o, way, 0, way, part_of(value, way))
        for o in (1, 0):
            for way in range(2):
                value = spread_right(n, xq(1 - 2 * way, o == 1))
                send(n, o, way, 1, 1 - way, part_of(value, 1 - way))
                keep[o, way, quarters(n)[way]] = part_of(value, way)

    def up_second(n):
        for o in (1, 0):
            for way in range(2):
                rows = quarters(n)[way]
                going[n, o, way, 0, way].wait_recv()
                send(n, o, way, 1, way, keep[o, way, rows] + srecv[o, way, 0, rows].astype(F32))

    def up_third(n, o):
        rows = pl.ds(256 * n, 256)
        value = spread_right(n, xq(0, o == 1))
        for way in range(2):
            for k in range(2):
                going[n, o, way, 1, k].wait_recv()
        for way in range(2):
            value += srecv[o, way, 1, rows].astype(F32)
        if o == 1:
            tsend[rows] = value.astype(BF16)
            last[n] = push(tsend.at[rows], trecv.at[rows], yh)
        else:
            last[n].wait_recv()
            update[rows] = value + trecv[rows].astype(F32)

    spread_left(zq(4))
    for n in range(2):
        for way in range(2):
            back_send(n, 1, way, way)
    spread_left(zq(3))
    spread_left(zq(-3))
    for n in range(2):
        for way in range(2):
            back_send(n, 2, way, 1 - way)
    spread_left(zq(2))
    spread_left(zq(-2))
    back_step(0, 2)
    spread_left(zq(1))
    spread_left(zq(-1))
    back_step(0, 3)
    back_step(1, 2)
    spread_left(z)
    back_step(0, 4)
    back_step(1, 3)
    back_step(1, 4)
    back_end(0)
    up_first(0)
    up_second(0)
    back_end(1)
    up_first(1)
    up_third(0, 1)
    up_second(1)
    up_third(0, 0)
    up_third(1, 1)
    up_third(1, 0)
    out_update = pltpu.make_async_copy(update, update_out, lsem.at[5])
    out_update.start()
    drain()
    out_avg.wait()
    out_sq.wait()
    out_update.wait()


def shards(grad, left_basis, right_basis, exp_avg, exp_avg_sq):
    block = jax.ShapeDtypeStruct((512, 256), F32)
    place = pl.BlockSpec(memory_space=pl.ANY)
    return pl.pallas_call(
        kernel,
        out_shape=(block, block, block),
        in_specs=[place] * 5,
        out_specs=(place,) * 3,
        scratch_shapes=[
            pltpu.VMEM((512, 256), F32),
            pltpu.VMEM((512, 256), F32),
            pltpu.VMEM((512, 256), F32),
            pltpu.VMEM((8, 512, 256), BF16),
            pltpu.VMEM((2, 8, 512, 512), BF16),
            pltpu.VMEM((8, 2, 256, 256), BF16),
            pltpu.VMEM((8, 512, 256), BF16),
            pltpu.VMEM((2, 512, 256), F32),
            pltpu.VMEM((512, 256), F32),
            pltpu.VMEM((2, 512, 256), F32),
            pltpu.VMEM((512, 256), F32),
            pltpu.VMEM((2, 512, 256), BF16),
            pltpu.VMEM((8, 512, 256), F32),
            pltpu.VMEM((2, 4, 512, 256), BF16),
            pltpu.VMEM((2, 4, 512, 256), BF16),
            pltpu.VMEM((2, 2, 2, 256, 256), BF16),
            pltpu.VMEM((2, 2, 2, 512, 256), BF16),
            pltpu.VMEM((2, 2, 2, 512, 256), BF16),
            pltpu.VMEM((2, 2, 512, 256), F32),
            pltpu.VMEM((512, 256), BF16),
            pltpu.VMEM((512, 256), BF16),
            pltpu.SemaphoreType.DMA((COPIES,)),
            pltpu.SemaphoreType.DMA((COPIES,)),
            pltpu.SemaphoreType.DMA((6,)),
        ],
        compiler_params=pltpu.CompilerParams(
            collective_id=0, has_side_effects=True, vmem_limit_bytes=56 * 1024 * 1024
        ),
        cost_estimate=pl.CostEstimate(flops=6_500_000_000, bytes_accessed=4_000_000, transcendentals=0),
    )(grad, left_basis, right_basis, exp_avg, exp_avg_sq)


def solution(mesh):
    return jax.shard_map(
        shards,
        mesh=mesh,
        in_specs=(
            P("row", "col"),
            P("col", "row"),
            P("row", "col"),
            P("row", "col"),
            P("row", "col"),
        ),
        out_specs=(P("row", "col"), P("row", "col"), P("row", "col")),
        check_vma=False,
    )
```

```python
import functools

import jax
import jax.numpy as jnp
from jax import lax
from jax.experimental import pallas as pl
from jax.experimental.pallas import tpu as pltpu
from jax.sharding import PartitionSpec as P

STEP = 10
beta_first = 0.95
beta_second = 0.95
epsilon = 1e-08

MESH = pl.DeviceIdType.MESH
F32 = jnp.float32
BF16 = jnp.bfloat16

COPIES = 160


def dot(a, b, dims):
    return lax.dot_general(a, b, (dims, ((), ())), preferred_element_type=F32)


NN = ((1,), (0,))
TN = ((0,), (0,))
NT = ((1,), (1,))


def kernel(
    g_ref, l_ref, r_ref, avg_in, sq_in,
    near_out, far_out, proj_out,
    update, avg, sq,
    gbuf, lbuf, rbuf, rot, part, part_in, proj, proj_in, dbuf,
    whole, wsend, wrecv, hilo, ssend, srecv, keep, opposite, tsend, trecv,
    ssem, rsem, lsem,
):
    row, col = lax.axis_index("row"), lax.axis_index("col")
    z, h = row // 2, row % 2
    x, t, j = col // 4, (col // 2) % 2, col % 2
    matched = h == j
    half = 256
    lo, hi = pl.ds(0, half), pl.ds(half, half)

    def zq(d):
        return (z + d + 8) % 8

    def xq(d, other):
        return 2 * ((x + d + 4) % 4) + (1 - t if other else t)

    zp, zm = (2 * zq(1) + h, col), (2 * zq(-1) + h, col)
    xp, xm = (row, (col + 4) % 16), (row, (col + 12) % 16)
    yh = (row, 4 * x + 2 * (1 - t) + j)
    yl = (2 * z + 1 - h, col)
    core = (row, 4 * x + 2 * t + 1 - j)
    diag = (2 * z + 1 - h, 4 * x + 2 * t + 1 - j)

    count = [0]
    sent = []

    def make(src, dst, who, slot=None):
        if slot is None:
            slot = count[0]
            count[0] += 1
        return pltpu.make_async_remote_copy(
            src_ref=src, dst_ref=dst, send_sem=ssem.at[slot], recv_sem=rsem.at[slot],
            device_id=who, device_id_type=MESH,
        )

    def push(src, dst, who):
        copy = make(src, dst, who)
        copy.start()
        sent.append(copy)
        return copy

    def later(src, dst, who):
        copy = make(src, dst, who)
        sent.append(copy)
        return copy

    def same(ref, who):
        return push(ref, ref, who)

    halves = ((0, 256), (256, 256))

    first = xq(0, False)
    own_g = pltpu.make_async_copy(g_ref, gbuf.at[z], lsem.at[0])
    own_l = pltpu.make_async_copy(l_ref, lbuf.at[j, first], lsem.at[1])
    r_own = pltpu.make_async_copy(r_ref, rbuf.at[z, j], lsem.at[2])
    swaps = [
        make(l_ref.at[pl.ds(*r)], lbuf.at[1 - j, first, pl.ds(*r)], diag) for r in halves
    ]

    keep_avg = pltpu.make_async_copy(avg_in, avg, lsem.at[3])
    keep_sq = pltpu.make_async_copy(sq_in, sq, lsem.at[4])
    own_g.start()
    keep_avg.start()
    keep_sq.start()

    @pl.when(matched)
    def _():
        own_l.start()
        r_own.start()

    barrier = pltpu.get_barrier_semaphore()
    for who in (zp, zm, xp, xm, yh, yl, core, diag):
        pl.semaphore_signal(barrier, inc=1, device_id=who, device_id_type=MESH)
    pl.semaphore_wait(barrier, 8)

    @pl.when(jnp.logical_not(matched))
    def _():
        for copy in swaps:
            copy.start()

    base_r = count[0]
    count[0] += 3
    r_far = make(r_ref, rbuf.at[z, j], (2 * z + 1 - h, 4 * x + 2 * t + h), base_r + j)
    r_near = make(r_ref, rbuf.at[z, j], core, base_r + 2)

    def drain():
        for copy in sent:
            copy.wait_send()
        r_far.wait_send()
        for ring in ring_rot:
            ring.far[0].wait_send()

        @pl.when(matched)
        def _():
            for ring in ring_l:
                ring.far[0].wait_send()

        @pl.when(jnp.logical_not(matched))
        def _():
            for ring in ring_l:
                for copy in ring.ring:
                    copy.wait_send()
            for copy in swaps:
                copy.wait_send()
            r_near.wait_send()

    class RingZ:
        def __init__(self, buf, cut):
            def both(k, low, high):
                return later(low, low, zp), later(high, high, zm)

            self.steps = [both(0, buf.at[z], buf.at[z])]
            for k in (1, 2, 3):
                low, high = buf.at[zq(-k)], buf.at[zq(k)]
                if k == 3:
                    low, high = cut(low, 0), cut(high, 1)
                self.steps.append(both(k, low, high))

        def start(self):
            for copy in self.steps[0]:
                copy.start()

        def step(self, k):
            for before, copy in zip(self.steps[k - 1], self.steps[k]):
                before.wait_recv()
                copy.start()

        def finish(self):
            for copy in self.steps[3]:
                copy.wait_recv()

    class RingX:
        def __init__(self, buf, top, size):
            low, high = pl.ds(top, size // 2), pl.ds(top + size // 2, size // 2)

            def to(q, rows, who):
                return later(buf.at[q, rows], buf.at[q, rows], who)

            self.y = to(xq(0, False), pl.ds(top, size), yh)
            self.lead, self.rest = {}, {}
            for other in (False, True):
                q = xq(0, other)
                self.lead[other] = to(q, low, xp), to(q, high, xm)
                self.rest[other] = to(q, high, xp), to(q, low, xm)
            self.passed = to(xq(-1, False), low, xp), to(xq(1, False), high, xm)
            down, up, far = xq(-1, True), xq(1, True), xq(2, False)
            whole_block = buf.at[far, pl.ds(top, size)]
            self.ring = (
                make(buf.at[down, low], buf.at[down, low], xp),
                make(buf.at[up, high], buf.at[up, high], xm),
            )
            self.far = (make(whole_block, whole_block, yh),)

        def across(self):
            self.y.start()

        def go(self, other):
            for copy in self.lead[other] + self.rest[other]:
                copy.start()

        def second(self):
            self.y.wait_recv()
            self.go(True)

        def forward(self):
            for before, copy in zip(self.lead[False], self.passed):
                before.wait_recv()
                copy.start()

        def forward_ring(self):
            for before, copy in zip(self.lead[True], self.ring):
                before.wait_recv()
                copy.start()

        def forward_far(self):
            for copy in self.passed:
                copy.wait_recv()
            self.far[0].start()

        def complete(self, *others):
            for other in others:
                for copy in self.rest[other]:
                    copy.wait_recv()

        def finish_far(self):
            for copy in self.lead[True] + self.rest[True] + self.far:
                copy.wait_recv()

    ring_g = RingZ(gbuf, lambda ref, k: ref.at[lo if k == 0 else hi])
    ring_r = RingZ(rbuf, lambda ref, k: ref.at[k])
    ring_l = [RingX(lbuf.at[j], *r) for r in halves]

    order = [(0, False), (-1, False), (1, False), (2, False), (0, True), (-1, True), (1, True), (2, True)]
    shared = [later(lbuf.at[j, xq(*o)], lbuf.at[j, xq(*o)], core) for o in order]

    def share(*which):
        for n in which:
            shared[n].start()

    def take(*which):
        for n in which:
            shared[n].wait_recv()

    def left(event, *which):
        for ring in ring_l:
            getattr(ring, event)(*which)

    def rotate(i, first, number):
        def body(n, carry):
            q = 2 * ((x + n // 2 + first) % 4) + n % 2
            part[i] += dot(lbuf[i, q], gbuf[q], TN)
            return carry

        lax.fori_loop(0, number, body, 0)

    pieces = tuple((128 * n, 128) for n in range(4))
    exchange = [later(part.at[1 - h, pl.ds(*r)], part_in.at[pl.ds(*r)], yl) for r in pieces]

    def give():
        for copy in exchange:
            copy.start()

    part[...] = jnp.zeros_like(part)

    @pl.when(matched)
    def _():
        own_l.wait()
        left("go", False)
        share(0)
        own_g.wait()
        ring_g.start()
        left("forward")
        ring_g.step(1)
        left("complete", False)
        share(1, 2)
        left("across")
        r_far.start()
        ring_g.step(2)
        left("forward_far")
        share(3)
        ring_g.step(3)
        make(r_ref, rbuf.at[z, 1 - j], core, base_r + 2).wait_recv()
        r_own.wait()
        ring_r.start()
        take(0, 1, 2, 4, 5, 6)
        left("second")
        share(4)
        ring_g.finish()
        rotate(1 - h, 3, 6)
        take(3, 7)
        rotate(1 - h, 2, 2)
        give()
        ring_r.step(1)
        left("finish_far")
        share(5, 6, 7)
        rotate(h, 0, 8)
        ring_r.step(2)

    @pl.when(jnp.logical_not(matched))
    def _():
        own_g.wait()
        ring_g.start()
        for ring, copy in zip(ring_l, swaps):
            copy.wait_recv()
            ring.across()
            ring.go(False)
        share(0)
        ring_g.step(1)
        left("forward")
        left("second")
        share(4)
        r_far.start()
        r_near.start()
        left("complete", False)
        share(1, 2)
        ring_g.step(2)
        left("forward_ring")
        for ring in ring_l:
            for copy in ring.passed:
                copy.wait_recv()
        share(3)
        ring_g.step(3)
        left("complete", True)
        share(5, 6)
        make(r_ref, rbuf.at[z, 0], core, base_r).wait_recv()
        make(r_ref, rbuf.at[z, 1], core, base_r + 1).wait_recv()
        ring_r.start()
        for ring in ring_l:
            for copy in ring.ring:
                copy.wait_recv()
        share(7)
        ring_g.finish()
        rotate(1 - h, 0, 8)
        give()
        ring_r.step(1)
        take(0, 1, 2, 4, 5, 6)
        rotate(h, 3, 6)
        take(3, 7)
        rotate(h, 2, 2)
        ring_r.step(2)


    ring_rot = [RingX(rot, *r) for r in halves]
    for n, r in enumerate(halves):
        exchange[2 * n].wait_recv()
        exchange[2 * n + 1].wait_recv()
        rows = pl.ds(*r)
        rot[first, rows] = (part[h, rows] + part_in[rows]).astype(BF16)
        ring_rot[n].across()
        ring_rot[n].go(False)
    ring_rot[0].forward()
    ring_rot[0].second()
    ring_r.step(3)
    ring_rot[1].forward()
    ring_rot[1].second()
    ring_rot[0].forward_far()
    ring_rot[1].forward_far()
    ring_rot[0].complete(False)
    ring_rot[0].finish_far()
    ring_r.finish()

    keep_avg.wait()
    keep_sq.wait()
    first_fix = 1.0 - beta_first**STEP
    second_fix = 1.0 - beta_second**STEP
    give_d = []
    for n, r in enumerate(halves):
        rows = pl.ds(*r)
        if n == 1:
            ring_rot[1].complete(False)
            ring_rot[1].finish_far()
        proj[:, rows] = jnp.zeros((2, 256, 256), F32)

        def project(q, carry):
            for c in range(2):
                proj[c, rows] += dot(rot[q, rows], rbuf[q, c], NN)
            return carry

        lax.fori_loop(0, 8, project, 0)
        push(proj.at[1 - j, rows], proj_in.at[rows], core).wait_recv()
        projected = proj[j, rows] + proj_in[rows]
        new_avg = beta_first * avg[rows] + (1.0 - beta_first) * projected
        new_sq = beta_second * sq[rows] + (1.0 - beta_second) * projected * projected
        proj_in[rows] = projected
        dbuf[h, rows] = (
            new_avg / first_fix / (jnp.sqrt(new_sq / second_fix) + epsilon)
        ).astype(BF16)
        give_d.append(same(dbuf.at[h, rows], yl))
    out_proj = pltpu.make_async_copy(proj_in, proj_out, lsem.at[3])
    out_proj.start()
    for copy in give_d:
        copy.wait_recv()

    def quarters(n):
        return (pl.ds(256 * n, 128), pl.ds(256 * n + 128, 128))

    def spread_left(q):
        whole[q] = dot(lbuf[0, q], dbuf[0], NN) + dot(lbuf[1, q], dbuf[1], NN)

    flying = {}

    def back_send(n, s, way, k):
        rows = quarters(n)[k]
        value = whole[zq(5 - s if way == 0 else s - 5), rows]
        before = flying.get((n, way, s - 1, k))
        if before is not None:
            before.wait_recv()
            value += wrecv[way, s - 2, rows].astype(F32)
        wsend[way, s - 1, rows] = value.astype(BF16)
        flying[n, way, s, k] = push(
            wsend.at[way, s - 1, rows], wrecv.at[way, s - 1, rows], (zp, zm)[way]
        )

    def back_step(n, s):
        for k in (0, 1):
            for way in (0, 1):
                if s > 2 or k == 0:
                    back_send(n, s, way, (1 - way, way)[k] if s > 2 else way)

    def back_end(n):
        rows = pl.ds(256 * n, 256)
        value = whole[z, rows]
        for way in range(2):
            for k in range(2):
                flying[n, way, 4, k].wait_recv()
        for way in range(2):
            value += wrecv[way, 3, rows].astype(F32)
        high = value.astype(BF16)
        hilo[n, j, 0] = high
        hilo[n, j, 1] = (value - high.astype(F32)).astype(BF16)
        push(hilo.at[n, j], hilo.at[n, j], core).wait_recv()

    def spread_right(n, q):
        total = dot(hilo[n, 0].reshape(512, 256), rbuf[q, 0], NT)
        total += dot(hilo[n, 1].reshape(512, 256), rbuf[q, 1], NT)
        return total[:256] + total[256:]

    going, last = {}, {}

    def send(key, slot, n, k, value):
        rows = pl.ds(256 * n, 256) if k is None else quarters(n)[k]
        ssend[slot, rows] = value.astype(BF16)
        going[key] = push(
            ssend.at[slot, rows], srecv.at[slot, rows], yh if slot == 0 else (xp, xm)[slot % 2 == 0]
        )

    def part_of(value, k):
        return value[128 * k : 128 * k + 128]

    def up_first(n):
        send((n, 0), 0, n, None, spread_right(n, xq(2, True)))
        for way in range(2):
            send((n, 1 + way), 1 + way, n, None, spread_right(n, xq(1 - 2 * way, True)))
        for way in range(2):
            value = spread_right(n, xq(1 - 2 * way, False))
            send((n, 3 + way, 1 - way), 3 + way, n, 1 - way, part_of(value, 1 - way))
            keep[way, quarters(n)[way]] = part_of(value, way)
        opposite[n] = spread_right(n, xq(2, False))

    def up_second(n):
        going[n, 0].wait_recv()
        for way in range(2):
            rows = quarters(n)[way]
            value = opposite[n, 128 * way : 128 * way + 128] + srecv[0, rows].astype(F32)
            send((n, 5 + way), 5 + way, n, way, value)

    def up_third(n):
        rows = pl.ds(256 * n, 256)
        value = spread_right(n, xq(0, True))
        for way in range(2):
            going[n, 1 + way].wait_recv()
            value += srecv[1 + way, rows].astype(F32)
        tsend[rows] = value.astype(BF16)
        last[n] = push(tsend.at[rows], trecv.at[rows], yh)

    def up_fourth(n):
        for way in range(2):
            rows = quarters(n)[way]
            going[n, 5 + way].wait_recv()
            send((n, 3 + way, way), 3 + way, n, way, keep[way, rows] + srecv[5 + way, rows].astype(F32))

    def up_last(n):
        rows = pl.ds(256 * n, 256)
        value = spread_right(n, xq(0, False))
        for way in range(2):
            for k in range(2):
                going[n, 3 + way, k].wait_recv()
            value += srecv[3 + way, rows].astype(F32)
        update[rows] = value

    def back_open(s):
        for n in range(2):
            for way in range(2):
                back_send(n, s, way, way if s == 1 else 1 - way)

    spread_left(zq(4))
    back_open(1)
    spread_left(zq(3))
    spread_left(zq(-3))
    back_open(2)
    spread_left(zq(2))
    spread_left(zq(-2))
    back_step(0, 2)
    back_step(1, 2)
    spread_left(zq(1))
    spread_left(zq(-1))
    back_step(0, 3)
    back_step(1, 3)
    spread_left(z)
    back_step(0, 4)
    back_step(1, 4)
    back_end(0)
    up_first(0)
    back_end(1)
    up_first(1)
    up_second(0)
    up_third(0)
    up_second(1)
    up_fourth(0)
    up_third(1)
    up_last(0)
    up_fourth(1)
    up_last(1)
    out_near = pltpu.make_async_copy(update, near_out, lsem.at[4])
    out_near.start()
    for n in range(2):
        last[n].wait_recv()
    out_far = pltpu.make_async_copy(trecv, far_out, lsem.at[5])
    out_far.start()
    drain()
    out_proj.wait()
    out_near.wait()
    out_far.wait()


def shards(grad, left_basis, right_basis, exp_avg, exp_avg_sq):
    block = jax.ShapeDtypeStruct((512, 256), F32)
    place = pl.BlockSpec(memory_space=pl.ANY)
    near, far, projected = pl.pallas_call(
        kernel,
        out_shape=(block, jax.ShapeDtypeStruct((512, 256), BF16), block),
        in_specs=[place] * 5,
        out_specs=(place,) * 3,
        scratch_shapes=[
            pltpu.VMEM((512, 256), F32),
            pltpu.VMEM((512, 256), F32),
            pltpu.VMEM((512, 256), F32),
            pltpu.VMEM((8, 512, 256), BF16),
            pltpu.VMEM((2, 8, 512, 512), BF16),
            pltpu.VMEM((8, 2, 256, 256), BF16),
            pltpu.VMEM((8, 512, 256), BF16),
            pltpu.VMEM((2, 512, 256), F32),
            pltpu.VMEM((512, 256), F32),
            pltpu.VMEM((2, 512, 256), F32),
            pltpu.VMEM((512, 256), F32),
            pltpu.VMEM((2, 512, 256), BF16),
            pltpu.VMEM((8, 512, 256), F32),
            pltpu.VMEM((2, 4, 512, 256), BF16),
            pltpu.VMEM((2, 4, 512, 256), BF16),
            pltpu.VMEM((2, 2, 2, 256, 256), BF16),
            pltpu.VMEM((7, 512, 256), BF16),
            pltpu.VMEM((7, 512, 256), BF16),
            pltpu.VMEM((2, 512, 256), F32),
            pltpu.VMEM((2, 256, 256), F32),
            pltpu.VMEM((512, 256), BF16),
            pltpu.VMEM((512, 256), BF16),
            pltpu.SemaphoreType.DMA((COPIES,)),
            pltpu.SemaphoreType.DMA((COPIES,)),
            pltpu.SemaphoreType.DMA((6,)),
        ],
        compiler_params=pltpu.CompilerParams(
            collective_id=0, has_side_effects=True, vmem_limit_bytes=56 * 1024 * 1024
        ),
        cost_estimate=pl.CostEstimate(flops=6_500_000_000, bytes_accessed=4_000_000, transcendentals=0),
    )(grad, left_basis, right_basis, exp_avg, exp_avg_sq)
    new_avg = beta_first * exp_avg + (1.0 - beta_first) * projected
    new_sq = beta_second * exp_avg_sq + (1.0 - beta_second) * projected * projected
    return near + far.astype(F32), new_avg, new_sq


def solution(mesh):
    return jax.shard_map(
        shards,
        mesh=mesh,
        in_specs=(
            P("row", "col"),
            P("col", "row"),
            P("row", "col"),
            P("row", "col"),
            P("row", "col"),
        ),
        out_specs=(P("row", "col"), P("row", "col"), P("row", "col")),
        check_vma=False,
    )
```

```python
import functools

import jax
import jax.numpy as jnp
from jax import lax
from jax.experimental import pallas as pl
from jax.experimental.pallas import tpu as pltpu
from jax.sharding import PartitionSpec as P

STEP = 10
beta_first = 0.95
beta_second = 0.95
epsilon = 1e-08

MESH = pl.DeviceIdType.MESH
F32 = jnp.float32
BF16 = jnp.bfloat16

COPIES = 160


def dot(a, b, dims):
    return lax.dot_general(a, b, (dims, ((), ())), preferred_element_type=F32)


NN = ((1,), (0,))
TN = ((0,), (0,))
NT = ((1,), (1,))


def kernel(
    g_ref, l_ref, r_ref, avg_in, sq_in,
    near_out, far_out, proj_out,
    update, avg, sq,
    gbuf, lbuf, rbuf, rot, part, part_in, proj, proj_in, dbuf,
    whole, wsend, wrecv, hilo, ssend, srecv, keep, opposite, tsend, trecv,
    ssem, rsem, lsem,
):
    row, col = lax.axis_index("row"), lax.axis_index("col")
    z, h = row // 2, row % 2
    x, t, j = col // 4, (col // 2) % 2, col % 2
    matched = h == j
    half = 256
    lo, hi = pl.ds(0, half), pl.ds(half, half)

    def zq(d):
        return (z + d + 8) % 8

    def xq(d, other):
        return 2 * ((x + d + 4) % 4) + (1 - t if other else t)

    zp, zm = (2 * zq(1) + h, col), (2 * zq(-1) + h, col)
    xp, xm = (row, (col + 4) % 16), (row, (col + 12) % 16)
    yh = (row, 4 * x + 2 * (1 - t) + j)
    yl = (2 * z + 1 - h, col)
    core = (row, 4 * x + 2 * t + 1 - j)
    diag = (2 * z + 1 - h, 4 * x + 2 * t + 1 - j)

    count = [0]
    sent = []

    def make(src, dst, who, slot=None):
        if slot is None:
            slot = count[0]
            count[0] += 1
        return pltpu.make_async_remote_copy(
            src_ref=src, dst_ref=dst, send_sem=ssem.at[slot], recv_sem=rsem.at[slot],
            device_id=who, device_id_type=MESH,
        )

    def push(src, dst, who):
        copy = make(src, dst, who)
        copy.start()
        sent.append(copy)
        return copy

    def later(src, dst, who):
        copy = make(src, dst, who)
        sent.append(copy)
        return copy

    def same(ref, who):
        return push(ref, ref, who)

    halves = ((0, 256), (256, 256))

    first = xq(0, False)
    own_g = pltpu.make_async_copy(g_ref, gbuf.at[z], lsem.at[0])
    own_l = pltpu.make_async_copy(l_ref, lbuf.at[j, first], lsem.at[1])
    r_own = pltpu.make_async_copy(r_ref, rbuf.at[z, j], lsem.at[2])
    swaps = [
        make(l_ref.at[pl.ds(*r)], lbuf.at[1 - j, first, pl.ds(*r)], diag) for r in halves
    ]

    keep_avg = pltpu.make_async_copy(avg_in, avg, lsem.at[3])
    keep_sq = pltpu.make_async_copy(sq_in, sq, lsem.at[4])
    own_g.start()
    keep_avg.start()
    keep_sq.start()

    @pl.when(matched)
    def _():
        own_l.start()
        r_own.start()

    barrier = pltpu.get_barrier_semaphore()
    for who in (zp, zm, xp, xm, yh, yl, core, diag):
        pl.semaphore_signal(barrier, inc=1, device_id=who, device_id_type=MESH)
    pl.semaphore_wait(barrier, 8)

    @pl.when(jnp.logical_not(matched))
    def _():
        for copy in swaps:
            copy.start()

    base_r = count[0]
    count[0] += 3
    r_far = make(r_ref, rbuf.at[z, j], (2 * z + 1 - h, 4 * x + 2 * t + h), base_r + j)
    r_near = make(r_ref, rbuf.at[z, j], core, base_r + 2)

    def drain():
        for copy in sent:
            copy.wait_send()
        r_far.wait_send()
        for ring in ring_rot:
            ring.far[0].wait_send()

        @pl.when(matched)
        def _():
            for ring in ring_l:
                ring.far[0].wait_send()

        @pl.when(jnp.logical_not(matched))
        def _():
            for ring in ring_l:
                for copy in ring.ring:
                    copy.wait_send()
            for copy in swaps:
                copy.wait_send()
            r_near.wait_send()

    class RingZ:
        def __init__(self, buf, cut):
            def both(k, low, high):
                return later(low, low, zp), later(high, high, zm)

            self.steps = [both(0, buf.at[z], buf.at[z])]
            for k in (1, 2, 3):
                low, high = buf.at[zq(-k)], buf.at[zq(k)]
                if k == 3:
                    low, high = cut(low, 0), cut(high, 1)
                self.steps.append(both(k, low, high))

        def start(self):
            for copy in self.steps[0]:
                copy.start()

        def step(self, k):
            for before, copy in zip(self.steps[k - 1], self.steps[k]):
                before.wait_recv()
                copy.start()

        def finish(self):
            for copy in self.steps[3]:
                copy.wait_recv()

    class RingX:
        def __init__(self, buf, top, size):
            low, high = pl.ds(top, size // 2), pl.ds(top + size // 2, size // 2)

            def to(q, rows, who):
                return later(buf.at[q, rows], buf.at[q, rows], who)

            self.y = to(xq(0, False), pl.ds(top, size), yh)
            self.lead, self.rest = {}, {}
            for other in (False, True):
                q = xq(0, other)
                self.lead[other] = to(q, low, xp), to(q, high, xm)
                self.rest[other] = to(q, high, xp), to(q, low, xm)
            self.passed = to(xq(-1, False), low, xp), to(xq(1, False), high, xm)
            down, up, far = xq(-1, True), xq(1, True), xq(2, False)
            whole_block = buf.at[far, pl.ds(top, size)]
            self.ring = (
                make(buf.at[down, low], buf.at[down, low], xp),
                make(buf.at[up, high], buf.at[up, high], xm),
            )
            self.far = (make(whole_block, whole_block, yh),)

        def across(self):
            self.y.start()

        def go(self, other):
            for copy in self.lead[other] + self.rest[other]:
                copy.start()

        def second(self):
            self.y.wait_recv()
            self.go(True)

        def forward(self):
            for before, copy in zip(self.lead[False], self.passed):
                before.wait_recv()
                copy.start()

        def forward_ring(self):
            for before, copy in zip(self.lead[True], self.ring):
                before.wait_recv()
                copy.start()

        def forward_far(self):
            for copy in self.passed:
                copy.wait_recv()
            self.far[0].start()

        def complete(self, *others):
            for other in others:
                for copy in self.rest[other]:
                    copy.wait_recv()

        def finish_far(self):
            for copy in self.lead[True] + self.rest[True] + self.far:
                copy.wait_recv()

    ring_g = RingZ(gbuf, lambda ref, k: ref.at[lo if k == 0 else hi])
    ring_r = RingZ(rbuf, lambda ref, k: ref.at[k])
    ring_l = [RingX(lbuf.at[j], *r) for r in halves]

    order = [(0, False), (-1, False), (1, False), (2, False), (0, True), (-1, True), (1, True), (2, True)]
    shared = [later(lbuf.at[j, xq(*o)], lbuf.at[j, xq(*o)], core) for o in order]

    def share(*which):
        for n in which:
            shared[n].start()

    def take(*which):
        for n in which:
            shared[n].wait_recv()

    def left(event, *which):
        for ring in ring_l:
            getattr(ring, event)(*which)

    def rotate(i, first, number):
        def body(n, carry):
            q = 2 * ((x + n // 2 + first) % 4) + n % 2
            part[i] += dot(lbuf[i, q], gbuf[q], TN)
            return carry

        lax.fori_loop(0, number, body, 0)

    pieces = tuple((128 * n, 128) for n in range(4))
    exchange = [later(part.at[1 - h, pl.ds(*r)], part_in.at[pl.ds(*r)], yl) for r in pieces]

    def give():
        for copy in exchange:
            copy.start()

    part[...] = jnp.zeros_like(part)

    @pl.when(matched)
    def _():
        own_l.wait()
        left("go", False)
        share(0)
        own_g.wait()
        ring_g.start()
        left("forward")
        ring_g.step(1)
        left("complete", False)
        share(1, 2)
        left("across")
        r_far.start()
        ring_g.step(2)
        left("forward_far")
        share(3)
        ring_g.step(3)
        make(r_ref, rbuf.at[z, 1 - j], core, base_r + 2).wait_recv()
        r_own.wait()
        ring_r.start()
        take(0, 1, 2, 4, 5, 6)
        left("second")
        share(4)
        ring_g.finish()
        rotate(1 - h, 3, 6)
        take(3, 7)
        rotate(1 - h, 2, 2)
        give()
        left("finish_far")
        share(5, 6, 7)
        ring_r.step(1)
        rotate(h, 0, 8)
        ring_r.step(2)

    @pl.when(jnp.logical_not(matched))
    def _():
        own_g.wait()
        ring_g.start()
        for ring, copy in zip(ring_l, swaps):
            copy.wait_recv()
            ring.across()
            ring.go(False)
        share(0)
        ring_g.step(1)
        left("forward")
        left("second")
        share(4)
        r_far.start()
        r_near.start()
        left("complete", False)
        share(1, 2)
        ring_g.step(2)
        left("forward_ring")
        for ring in ring_l:
            for copy in ring.passed:
                copy.wait_recv()
        share(3)
        ring_g.step(3)
        left("complete", True)
        share(5, 6)
        make(r_ref, rbuf.at[z, 0], core, base_r).wait_recv()
        make(r_ref, rbuf.at[z, 1], core, base_r + 1).wait_recv()
        ring_r.start()
        for ring in ring_l:
            for copy in ring.ring:
                copy.wait_recv()
        share(7)
        ring_g.finish()
        rotate(1 - h, 0, 8)
        give()
        ring_r.step(1)
        take(0, 1, 2, 4, 5, 6)
        rotate(h, 3, 6)
        take(3, 7)
        rotate(h, 2, 2)
        ring_r.step(2)


    ring_rot = [RingX(rot, *r) for r in halves]
    for n, r in enumerate(halves):
        exchange[2 * n].wait_recv()
        exchange[2 * n + 1].wait_recv()
        rows = pl.ds(*r)
        rot[first, rows] = (part[h, rows] + part_in[rows]).astype(BF16)
        ring_rot[n].across()
        ring_rot[n].go(False)
    ring_rot[0].forward()
    ring_rot[0].second()
    ring_r.step(3)
    ring_rot[1].forward()
    ring_rot[1].second()
    ring_rot[0].forward_far()
    ring_rot[1].forward_far()
    ring_rot[0].complete(False)
    ring_rot[0].finish_far()
    ring_r.finish()

    keep_avg.wait()
    keep_sq.wait()
    first_fix = 1.0 - beta_first**STEP
    second_fix = 1.0 - beta_second**STEP
    give_d = []
    for n, r in enumerate(halves):
        rows = pl.ds(*r)
        if n == 1:
            ring_rot[1].complete(False)
            ring_rot[1].finish_far()
        proj[:, rows] = jnp.zeros((2, 256, 256), F32)

        def project(q, carry):
            for c in range(2):
                proj[c, rows] += dot(rot[q, rows], rbuf[q, c], NN)
            return carry

        lax.fori_loop(0, 8, project, 0)
        push(proj.at[1 - j, rows], proj_in.at[rows], core).wait_recv()
        projected = proj[j, rows] + proj_in[rows]
        new_avg = beta_first * avg[rows] + (1.0 - beta_first) * projected
        new_sq = beta_second * sq[rows] + (1.0 - beta_second) * projected * projected
        proj_in[rows] = projected
        dbuf[h, rows] = (
            new_avg / first_fix / (jnp.sqrt(new_sq / second_fix) + epsilon)
        ).astype(BF16)
        give_d.append(same(dbuf.at[h, rows], yl))
    out_proj = pltpu.make_async_copy(proj_in, proj_out, lsem.at[3])
    out_proj.start()
    for copy in give_d:
        copy.wait_recv()

    def quarters(n):
        return (pl.ds(256 * n, 128), pl.ds(256 * n + 128, 128))

    def spread_left(q):
        whole[q] = dot(lbuf[0, q], dbuf[0], NN) + dot(lbuf[1, q], dbuf[1], NN)

    flying = {}

    def back_send(n, s, way, k):
        rows = quarters(n)[k]
        value = whole[zq(5 - s if way == 0 else s - 5), rows]
        before = flying.get((n, way, s - 1, k))
        if before is not None:
            before.wait_recv()
            value += wrecv[way, s - 2, rows].astype(F32)
        wsend[way, s - 1, rows] = value.astype(BF16)
        flying[n, way, s, k] = push(
            wsend.at[way, s - 1, rows], wrecv.at[way, s - 1, rows], (zp, zm)[way]
        )

    def back_step(n, s):
        for k in (0, 1):
            for way in (0, 1):
                if s > 2 or k == 0:
                    back_send(n, s, way, (1 - way, way)[k] if s > 2 else way)

    def back_end(n):
        rows = pl.ds(256 * n, 256)
        value = whole[z, rows]
        for way in range(2):
            for k in range(2):
                flying[n, way, 4, k].wait_recv()
        for way in range(2):
            value += wrecv[way, 3, rows].astype(F32)
        high = value.astype(BF16)
        hilo[n, j, 0] = high
        hilo[n, j, 1] = (value - high.astype(F32)).astype(BF16)
        push(hilo.at[n, j], hilo.at[n, j], core).wait_recv()

    def spread_right(n, q):
        total = dot(hilo[n, 0].reshape(512, 256), rbuf[q, 0], NT)
        total += dot(hilo[n, 1].reshape(512, 256), rbuf[q, 1], NT)
        return total[:256] + total[256:]

    going, last = {}, {}

    def send(key, slot, n, k, value):
        rows = pl.ds(256 * n, 256) if k is None else quarters(n)[k]
        ssend[slot, rows] = value.astype(BF16)
        going[key] = push(
            ssend.at[slot, rows], srecv.at[slot, rows], yh if slot == 0 else (xp, xm)[slot % 2 == 0]
        )

    def part_of(value, k):
        return value[128 * k : 128 * k + 128]

    def up_first(n):
        send((n, 0), 0, n, None, spread_right(n, xq(2, True)))
        for way in range(2):
            send((n, 1 + way), 1 + way, n, None, spread_right(n, xq(1 - 2 * way, True)))
        for way in range(2):
            value = spread_right(n, xq(1 - 2 * way, False))
            send((n, 3 + way, 1 - way), 3 + way, n, 1 - way, part_of(value, 1 - way))
            keep[way, quarters(n)[way]] = part_of(value, way)
        opposite[n] = spread_right(n, xq(2, False))

    def up_second(n):
        going[n, 0].wait_recv()
        for way in range(2):
            rows = quarters(n)[way]
            value = opposite[n, 128 * way : 128 * way + 128] + srecv[0, rows].astype(F32)
            send((n, 5 + way), 5 + way, n, way, value)

    def up_third(n):
        rows = pl.ds(256 * n, 256)
        value = spread_right(n, xq(0, True))
        for way in range(2):
            going[n, 1 + way].wait_recv()
            value += srecv[1 + way, rows].astype(F32)
        tsend[rows] = value.astype(BF16)
        last[n] = push(tsend.at[rows], trecv.at[rows], yh)

    def up_fourth(n):
        for way in range(2):
            rows = quarters(n)[way]
            going[n, 5 + way].wait_recv()
            send((n, 3 + way, way), 3 + way, n, way, keep[way, rows] + srecv[5 + way, rows].astype(F32))

    def up_last(n):
        rows = pl.ds(256 * n, 256)
        value = spread_right(n, xq(0, False))
        for way in range(2):
            for k in range(2):
                going[n, 3 + way, k].wait_recv()
            value += srecv[3 + way, rows].astype(F32)
        update[rows] = value

    def back_open(s):
        for n in range(2):
            for way in range(2):
                back_send(n, s, way, way if s == 1 else 1 - way)

    spread_left(zq(4))
    back_open(1)
    spread_left(zq(3))
    spread_left(zq(-3))
    back_open(2)
    spread_left(zq(2))
    spread_left(zq(-2))
    back_step(0, 2)
    back_step(1, 2)
    spread_left(zq(1))
    spread_left(zq(-1))
    back_step(0, 3)
    back_step(1, 3)
    spread_left(z)
    back_step(0, 4)
    back_step(1, 4)
    back_end(0)
    up_first(0)
    back_end(1)
    up_first(1)
    up_second(0)
    up_third(0)
    up_second(1)
    up_fourth(0)
    up_third(1)
    up_last(0)
    up_fourth(1)
    up_last(1)
    out_near = pltpu.make_async_copy(update, near_out, lsem.at[4])
    out_near.start()
    for n in range(2):
        last[n].wait_recv()
    out_far = pltpu.make_async_copy(trecv, far_out, lsem.at[5])
    out_far.start()
    drain()
    out_proj.wait()
    out_near.wait()
    out_far.wait()


def shards(grad, left_basis, right_basis, exp_avg, exp_avg_sq):
    block = jax.ShapeDtypeStruct((512, 256), F32)
    place = pl.BlockSpec(memory_space=pl.ANY)
    near, far, projected = pl.pallas_call(
        kernel,
        out_shape=(block, jax.ShapeDtypeStruct((512, 256), BF16), block),
        in_specs=[place] * 5,
        out_specs=(place,) * 3,
        scratch_shapes=[
            pltpu.VMEM((512, 256), F32),
            pltpu.VMEM((512, 256), F32),
            pltpu.VMEM((512, 256), F32),
            pltpu.VMEM((8, 512, 256), BF16),
            pltpu.VMEM((2, 8, 512, 512), BF16),
            pltpu.VMEM((8, 2, 256, 256), BF16),
            pltpu.VMEM((8, 512, 256), BF16),
            pltpu.VMEM((2, 512, 256), F32),
            pltpu.VMEM((512, 256), F32),
            pltpu.VMEM((2, 512, 256), F32),
            pltpu.VMEM((512, 256), F32),
            pltpu.VMEM((2, 512, 256), BF16),
            pltpu.VMEM((8, 512, 256), F32),
            pltpu.VMEM((2, 4, 512, 256), BF16),
            pltpu.VMEM((2, 4, 512, 256), BF16),
            pltpu.VMEM((2, 2, 2, 256, 256), BF16),
            pltpu.VMEM((7, 512, 256), BF16),
            pltpu.VMEM((7, 512, 256), BF16),
            pltpu.VMEM((2, 512, 256), F32),
            pltpu.VMEM((2, 256, 256), F32),
            pltpu.VMEM((512, 256), BF16),
            pltpu.VMEM((512, 256), BF16),
            pltpu.SemaphoreType.DMA((COPIES,)),
            pltpu.SemaphoreType.DMA((COPIES,)),
            pltpu.SemaphoreType.DMA((6,)),
        ],
        compiler_params=pltpu.CompilerParams(
            collective_id=0, has_side_effects=True, vmem_limit_bytes=56 * 1024 * 1024
        ),
        cost_estimate=pl.CostEstimate(flops=6_500_000_000, bytes_accessed=4_000_000, transcendentals=0),
    )(grad, left_basis, right_basis, exp_avg, exp_avg_sq)
    new_avg = beta_first * exp_avg + (1.0 - beta_first) * projected
    new_sq = beta_second * exp_avg_sq + (1.0 - beta_second) * projected * projected
    return near + far.astype(F32), new_avg, new_sq


def solution(mesh):
    return jax.shard_map(
        shards,
        mesh=mesh,
        in_specs=(
            P("row", "col"),
            P("col", "row"),
            P("row", "col"),
            P("row", "col"),
            P("row", "col"),
        ),
        out_specs=(P("row", "col"), P("row", "col"), P("row", "col")),
        check_vma=False,
    )
```

```python
import functools

import jax
import jax.numpy as jnp
from jax import lax
from jax.experimental import pallas as pl
from jax.experimental.pallas import tpu as pltpu
from jax.sharding import PartitionSpec as P

STEP = 10
beta_first = 0.95
beta_second = 0.95
epsilon = 1e-08

MESH = pl.DeviceIdType.MESH
F32 = jnp.float32
BF16 = jnp.bfloat16

COPIES = 160


def dot(a, b, dims):
    return lax.dot_general(a, b, (dims, ((), ())), preferred_element_type=F32)


NN = ((1,), (0,))
TN = ((0,), (0,))
NT = ((1,), (1,))


def kernel(
    g_ref, l_ref, r_ref, avg_in, sq_in,
    near_out, far_out, proj_out,
    update, avg, sq,
    gbuf, lbuf, rbuf, rot, part, part_in, proj, proj_in, dbuf,
    whole, wsend, wrecv, hilo, ssend, srecv, keep, opposite, tsend, trecv,
    ssem, rsem, lsem,
):
    row, col = lax.axis_index("row"), lax.axis_index("col")
    z, h = row // 2, row % 2
    x, t, j = col // 4, (col // 2) % 2, col % 2
    matched = h == j
    half = 256
    lo, hi = pl.ds(0, half), pl.ds(half, half)

    def zq(d):
        return (z + d + 8) % 8

    def xq(d, other):
        return 2 * ((x + d + 4) % 4) + (1 - t if other else t)

    zp, zm = (2 * zq(1) + h, col), (2 * zq(-1) + h, col)
    xp, xm = (row, (col + 4) % 16), (row, (col + 12) % 16)
    yh = (row, 4 * x + 2 * (1 - t) + j)
    yl = (2 * z + 1 - h, col)
    core = (row, 4 * x + 2 * t + 1 - j)
    diag = (2 * z + 1 - h, 4 * x + 2 * t + 1 - j)

    count = [0]
    sent = []

    def make(src, dst, who, slot=None):
        if slot is None:
            slot = count[0]
            count[0] += 1
        return pltpu.make_async_remote_copy(
            src_ref=src, dst_ref=dst, send_sem=ssem.at[slot], recv_sem=rsem.at[slot],
            device_id=who, device_id_type=MESH,
        )

    def push(src, dst, who):
        copy = make(src, dst, who)
        copy.start()
        sent.append(copy)
        return copy

    def later(src, dst, who):
        copy = make(src, dst, who)
        sent.append(copy)
        return copy

    def same(ref, who):
        return push(ref, ref, who)

    halves = ((0, 256), (256, 256))

    first = xq(0, False)
    own_g = pltpu.make_async_copy(g_ref, gbuf.at[z], lsem.at[0])
    own_l = pltpu.make_async_copy(l_ref, lbuf.at[j, first], lsem.at[1])
    r_own = pltpu.make_async_copy(r_ref, rbuf.at[z, j], lsem.at[2])
    swaps = [
        make(l_ref.at[pl.ds(*r)], lbuf.at[1 - j, first, pl.ds(*r)], diag) for r in halves
    ]

    keep_avg = pltpu.make_async_copy(avg_in, avg, lsem.at[3])
    keep_sq = pltpu.make_async_copy(sq_in, sq, lsem.at[4])
    own_g.start()
    keep_avg.start()
    keep_sq.start()

    @pl.when(matched)
    def _():
        own_l.start()
        r_own.start()

    barrier = pltpu.get_barrier_semaphore()
    for who in (zp, zm, xp, xm, yh, yl, core, diag):
        pl.semaphore_signal(barrier, inc=1, device_id=who, device_id_type=MESH)
    pl.semaphore_wait(barrier, 8)

    @pl.when(jnp.logical_not(matched))
    def _():
        for copy in swaps:
            copy.start()

    base_r = count[0]
    count[0] += 3
    r_far = make(r_ref, rbuf.at[z, j], (2 * z + 1 - h, 4 * x + 2 * t + h), base_r + j)
    r_near = make(r_ref, rbuf.at[z, j], core, base_r + 2)

    def drain():
        for copy in sent:
            copy.wait_send()
        r_far.wait_send()
        for ring in ring_rot:
            ring.far[0].wait_send()

        @pl.when(matched)
        def _():
            for ring in ring_l:
                ring.far[0].wait_send()

        @pl.when(jnp.logical_not(matched))
        def _():
            for ring in ring_l:
                for copy in ring.ring:
                    copy.wait_send()
            for copy in swaps:
                copy.wait_send()
            r_near.wait_send()

    class RingZ:
        def __init__(self, buf, cut):
            def both(k, low, high):
                return later(low, low, zp), later(high, high, zm)

            self.steps = [both(0, buf.at[z], buf.at[z])]
            for k in (1, 2, 3):
                low, high = buf.at[zq(-k)], buf.at[zq(k)]
                if k == 3:
                    low, high = cut(low, 0), cut(high, 1)
                self.steps.append(both(k, low, high))

        def start(self):
            for copy in self.steps[0]:
                copy.start()

        def step(self, k):
            for before, copy in zip(self.steps[k - 1], self.steps[k]):
                before.wait_recv()
                copy.start()

        def finish(self):
            for copy in self.steps[3]:
                copy.wait_recv()

    class RingX:
        def __init__(self, buf, top, size):
            low, high = pl.ds(top, size // 2), pl.ds(top + size // 2, size // 2)

            def to(q, rows, who):
                return later(buf.at[q, rows], buf.at[q, rows], who)

            self.y = to(xq(0, False), pl.ds(top, size), yh)
            self.lead, self.rest = {}, {}
            for other in (False, True):
                q = xq(0, other)
                self.lead[other] = to(q, low, xp), to(q, high, xm)
                self.rest[other] = to(q, high, xp), to(q, low, xm)
            self.passed = to(xq(-1, False), low, xp), to(xq(1, False), high, xm)
            down, up, far = xq(-1, True), xq(1, True), xq(2, False)
            whole_block = buf.at[far, pl.ds(top, size)]
            self.ring = (
                make(buf.at[down, low], buf.at[down, low], xp),
                make(buf.at[up, high], buf.at[up, high], xm),
            )
            self.far = (make(whole_block, whole_block, yh),)

        def across(self):
            self.y.start()

        def go(self, other):
            for copy in self.lead[other] + self.rest[other]:
                copy.start()

        def second(self):
            self.y.wait_recv()
            self.go(True)

        def forward(self):
            for before, copy in zip(self.lead[False], self.passed):
                before.wait_recv()
                copy.start()

        def forward_ring(self):
            for before, copy in zip(self.lead[True], self.ring):
                before.wait_recv()
                copy.start()

        def forward_far(self):
            for copy in self.passed:
                copy.wait_recv()
            self.far[0].start()

        def complete(self, *others):
            for other in others:
                for copy in self.rest[other]:
                    copy.wait_recv()

        def finish_far(self):
            for copy in self.lead[True] + self.rest[True] + self.far:
                copy.wait_recv()

    ring_g = RingZ(gbuf, lambda ref, k: ref.at[lo if k == 0 else hi])
    ring_r = RingZ(rbuf, lambda ref, k: ref.at[k])
    ring_l = [RingX(lbuf.at[j], *r) for r in halves]

    order = [(0, False), (-1, False), (1, False), (2, False), (0, True), (-1, True), (1, True), (2, True)]
    shared = [later(lbuf.at[j, xq(*o)], lbuf.at[j, xq(*o)], core) for o in order]

    def share(*which):
        for n in which:
            shared[n].start()

    def take(*which):
        for n in which:
            shared[n].wait_recv()

    def left(event, *which):
        for ring in ring_l:
            getattr(ring, event)(*which)

    def rotate(i, first, number):
        def body(n, carry):
            q = 2 * ((x + n // 2 + first) % 4) + n % 2
            part[i] += dot(lbuf[i, q], gbuf[q], TN)
            return carry

        lax.fori_loop(0, number, body, 0)

    pieces = tuple((128 * n, 128) for n in range(4))
    exchange = [later(part.at[1 - h, pl.ds(*r)], part_in.at[pl.ds(*r)], yl) for r in pieces]

    def give():
        for copy in exchange:
            copy.start()

    part[...] = jnp.zeros_like(part)

    @pl.when(matched)
    def _():
        own_l.wait()
        left("go", False)
        share(0)
        own_g.wait()
        ring_g.start()
        left("forward")
        ring_g.step(1)
        left("complete", False)
        share(1, 2)
        left("across")
        r_far.start()
        ring_g.step(2)
        left("forward_far")
        share(3)
        ring_g.step(3)
        make(r_ref, rbuf.at[z, 1 - j], core, base_r + 2).wait_recv()
        r_own.wait()
        ring_r.start()
        take(0, 1, 2, 4, 5, 6)
        left("second")
        share(4)
        ring_g.finish()
        rotate(1 - h, 3, 6)
        take(3, 7)
        rotate(1 - h, 2, 2)
        give()
        left("finish_far")
        share(5, 6, 7)
        ring_r.step(1)
        rotate(h, 0, 8)
        ring_r.step(2)

    @pl.when(jnp.logical_not(matched))
    def _():
        own_g.wait()
        ring_g.start()
        for ring, copy in zip(ring_l, swaps):
            copy.wait_recv()
            ring.across()
            ring.go(False)
        share(0)
        ring_g.step(1)
        left("forward")
        left("second")
        share(4)
        r_far.start()
        r_near.start()
        left("complete", False)
        share(1, 2)
        ring_g.step(2)
        left("forward_ring")
        for ring in ring_l:
            for copy in ring.passed:
                copy.wait_recv()
        share(3)
        ring_g.step(3)
        left("complete", True)
        share(5, 6)
        make(r_ref, rbuf.at[z, 0], core, base_r).wait_recv()
        make(r_ref, rbuf.at[z, 1], core, base_r + 1).wait_recv()
        ring_r.start()
        for ring in ring_l:
            for copy in ring.ring:
                copy.wait_recv()
        share(7)
        ring_g.finish()
        rotate(1 - h, 0, 8)
        give()
        ring_r.step(1)
        take(0, 1, 2, 4, 5, 6)
        rotate(h, 3, 6)
        take(3, 7)
        rotate(h, 2, 2)
        ring_r.step(2)


    ring_rot = [RingX(rot, *r) for r in halves]
    for n, r in enumerate(halves):
        exchange[2 * n].wait_recv()
        exchange[2 * n + 1].wait_recv()
        rows = pl.ds(*r)
        rot[first, rows] = (part[h, rows] + part_in[rows]).astype(BF16)
        ring_rot[n].across()
        ring_rot[n].go(False)
    ring_rot[0].forward()
    ring_rot[0].second()
    ring_r.step(3)
    ring_rot[1].forward()
    ring_rot[1].second()
    ring_rot[0].forward_far()
    ring_rot[1].forward_far()
    ring_r.finish()

    keep_avg.wait()
    keep_sq.wait()
    first_fix = 1.0 - beta_first**STEP
    second_fix = 1.0 - beta_second**STEP
    give_d = []
    for n, r in enumerate(halves):
        rows = pl.ds(*r)
        proj[:, rows] = jnp.zeros((2, 256, 256), F32)

        def project(other):
            def body(m, carry):
                q = 2 * ((x + m) % 4) + (1 - t if other else t)
                for c in range(2):
                    proj[c, rows] += dot(rot[q, rows], rbuf[q, c], NN)
                return carry

            lax.fori_loop(0, 4, body, 0)

        ring_rot[n].complete(False)
        project(False)
        ring_rot[n].finish_far()
        project(True)
        push(proj.at[1 - j, rows], proj_in.at[rows], core).wait_recv()
        projected = proj[j, rows] + proj_in[rows]
        new_avg = beta_first * avg[rows] + (1.0 - beta_first) * projected
        new_sq = beta_second * sq[rows] + (1.0 - beta_second) * projected * projected
        proj_in[rows] = projected
        dbuf[h, rows] = (
            new_avg / first_fix / (jnp.sqrt(new_sq / second_fix) + epsilon)
        ).astype(BF16)
        give_d.append(same(dbuf.at[h, rows], yl))
    out_proj = pltpu.make_async_copy(proj_in, proj_out, lsem.at[3])
    out_proj.start()
    for copy in give_d:
        copy.wait_recv()

    def quarters(n):
        return (pl.ds(256 * n, 128), pl.ds(256 * n + 128, 128))

    def spread_left(q):
        whole[q] = dot(lbuf[0, q], dbuf[0], NN) + dot(lbuf[1, q], dbuf[1], NN)

    flying = {}

    def back_send(n, s, way, k):
        rows = quarters(n)[k]
        value = whole[zq(5 - s if way == 0 else s - 5), rows]
        before = flying.get((n, way, s - 1, k))
        if before is not None:
            before.wait_recv()
            value += wrecv[way, s - 2, rows].astype(F32)
        wsend[way, s - 1, rows] = value.astype(BF16)
        flying[n, way, s, k] = push(
            wsend.at[way, s - 1, rows], wrecv.at[way, s - 1, rows], (zp, zm)[way]
        )

    def back_step(n, s):
        for k in (0, 1):
            for way in (0, 1):
                if s > 2 or k == 0:
                    back_send(n, s, way, (1 - way, way)[k] if s > 2 else way)

    def back_end(n):
        rows = pl.ds(256 * n, 256)
        value = whole[z, rows]
        for way in range(2):
            for k in range(2):
                flying[n, way, 4, k].wait_recv()
        for way in range(2):
            value += wrecv[way, 3, rows].astype(F32)
        high = value.astype(BF16)
        hilo[n, j, 0] = high
        hilo[n, j, 1] = (value - high.astype(F32)).astype(BF16)
        push(hilo.at[n, j], hilo.at[n, j], core).wait_recv()

    def spread_right(n, q):
        total = dot(hilo[n, 0].reshape(512, 256), rbuf[q, 0], NT)
        total += dot(hilo[n, 1].reshape(512, 256), rbuf[q, 1], NT)
        return total[:256] + total[256:]

    going, last = {}, {}

    def send(key, slot, n, k, value):
        rows = pl.ds(256 * n, 256) if k is None else quarters(n)[k]
        ssend[slot, rows] = value.astype(BF16)
        going[key] = push(
            ssend.at[slot, rows], srecv.at[slot, rows], yh if slot == 0 else (xp, xm)[slot % 2 == 0]
        )

    def part_of(value, k):
        return value[128 * k : 128 * k + 128]

    def up_first(n):
        send((n, 0), 0, n, None, spread_right(n, xq(2, True)))
        for way in range(2):
            send((n, 1 + way), 1 + way, n, None, spread_right(n, xq(1 - 2 * way, True)))
        for way in range(2):
            value = spread_right(n, xq(1 - 2 * way, False))
            send((n, 3 + way, 1 - way), 3 + way, n, 1 - way, part_of(value, 1 - way))
            keep[way, quarters(n)[way]] = part_of(value, way)
        opposite[n] = spread_right(n, xq(2, False))

    def up_second(n):
        going[n, 0].wait_recv()
        for way in range(2):
            rows = quarters(n)[way]
            value = opposite[n, 128 * way : 128 * way + 128] + srecv[0, rows].astype(F32)
            send((n, 5 + way), 5 + way, n, way, value)

    def up_third(n):
        rows = pl.ds(256 * n, 256)
        value = spread_right(n, xq(0, True))
        for way in range(2):
            going[n, 1 + way].wait_recv()
            value += srecv[1 + way, rows].astype(F32)
        tsend[rows] = value.astype(BF16)
        last[n] = push(tsend.at[rows], trecv.at[rows], yh)

    def up_fourth(n):
        for way in range(2):
            rows = quarters(n)[way]
            going[n, 5 + way].wait_recv()
            send((n, 3 + way, way), 3 + way, n, way, keep[way, rows] + srecv[5 + way, rows].astype(F32))

    def up_last(n):
        rows = pl.ds(256 * n, 256)
        value = spread_right(n, xq(0, False))
        for way in range(2):
            for k in range(2):
                going[n, 3 + way, k].wait_recv()
            value += srecv[3 + way, rows].astype(F32)
        update[rows] = value

    def back_open(s):
        for n in range(2):
            for way in range(2):
                back_send(n, s, way, way if s == 1 else 1 - way)

    spread_left(zq(4))
    back_open(1)
    spread_left(zq(3))
    spread_left(zq(-3))
    back_open(2)
    spread_left(zq(2))
    spread_left(zq(-2))
    back_step(0, 2)
    back_step(1, 2)
    spread_left(zq(1))
    spread_left(zq(-1))
    back_step(0, 3)
    back_step(1, 3)
    spread_left(z)
    back_step(0, 4)
    back_step(1, 4)
    back_end(0)
    up_first(0)
    back_end(1)
    up_first(1)
    up_second(0)
    up_third(0)
    up_second(1)
    up_fourth(0)
    up_third(1)
    up_last(0)
    up_fourth(1)
    up_last(1)
    out_near = pltpu.make_async_copy(update, near_out, lsem.at[4])
    out_near.start()
    for n in range(2):
        last[n].wait_recv()
    out_far = pltpu.make_async_copy(trecv, far_out, lsem.at[5])
    out_far.start()
    drain()
    out_proj.wait()
    out_near.wait()
    out_far.wait()


def shards(grad, left_basis, right_basis, exp_avg, exp_avg_sq):
    block = jax.ShapeDtypeStruct((512, 256), F32)
    place = pl.BlockSpec(memory_space=pl.ANY)
    near, far, projected = pl.pallas_call(
        kernel,
        out_shape=(block, jax.ShapeDtypeStruct((512, 256), BF16), block),
        in_specs=[place] * 5,
        out_specs=(place,) * 3,
        scratch_shapes=[
            pltpu.VMEM((512, 256), F32),
            pltpu.VMEM((512, 256), F32),
            pltpu.VMEM((512, 256), F32),
            pltpu.VMEM((8, 512, 256), BF16),
            pltpu.VMEM((2, 8, 512, 512), BF16),
            pltpu.VMEM((8, 2, 256, 256), BF16),
            pltpu.VMEM((8, 512, 256), BF16),
            pltpu.VMEM((2, 512, 256), F32),
            pltpu.VMEM((512, 256), F32),
            pltpu.VMEM((2, 512, 256), F32),
            pltpu.VMEM((512, 256), F32),
            pltpu.VMEM((2, 512, 256), BF16),
            pltpu.VMEM((8, 512, 256), F32),
            pltpu.VMEM((2, 4, 512, 256), BF16),
            pltpu.VMEM((2, 4, 512, 256), BF16),
            pltpu.VMEM((2, 2, 2, 256, 256), BF16),
            pltpu.VMEM((7, 512, 256), BF16),
            pltpu.VMEM((7, 512, 256), BF16),
            pltpu.VMEM((2, 512, 256), F32),
            pltpu.VMEM((2, 256, 256), F32),
            pltpu.VMEM((512, 256), BF16),
            pltpu.VMEM((512, 256), BF16),
            pltpu.SemaphoreType.DMA((COPIES,)),
            pltpu.SemaphoreType.DMA((COPIES,)),
            pltpu.SemaphoreType.DMA((6,)),
        ],
        compiler_params=pltpu.CompilerParams(
            collective_id=0, has_side_effects=True, vmem_limit_bytes=56 * 1024 * 1024
        ),
        cost_estimate=pl.CostEstimate(flops=6_500_000_000, bytes_accessed=4_000_000, transcendentals=0),
    )(grad, left_basis, right_basis, exp_avg, exp_avg_sq)
    new_avg = beta_first * exp_avg + (1.0 - beta_first) * projected
    new_sq = beta_second * exp_avg_sq + (1.0 - beta_second) * projected * projected
    return near + far.astype(F32), new_avg, new_sq


def solution(mesh):
    return jax.shard_map(
        shards,
        mesh=mesh,
        in_specs=(
            P("row", "col"),
            P("col", "row"),
            P("row", "col"),
            P("row", "col"),
            P("row", "col"),
        ),
        out_specs=(P("row", "col"), P("row", "col"), P("row", "col")),
        check_vma=False,
    )
```

```python
import functools

import jax
import jax.numpy as jnp
from jax import lax
from jax.experimental import pallas as pl
from jax.experimental.pallas import tpu as pltpu
from jax.sharding import PartitionSpec as P

STEP = 10
beta_first = 0.95
beta_second = 0.95
epsilon = 1e-08

MESH = pl.DeviceIdType.MESH
F32 = jnp.float32
BF16 = jnp.bfloat16

COPIES = 160


def dot(a, b, dims):
    return lax.dot_general(a, b, (dims, ((), ())), preferred_element_type=F32)


NN = ((1,), (0,))
TN = ((0,), (0,))
NT = ((1,), (1,))


def kernel(
    g_ref, l_ref, r_ref, avg_in, sq_in,
    near_out, far_out, proj_out,
    update, avg, sq,
    gbuf, lbuf, rbuf, rot, part, part_in, proj, proj_in, dbuf,
    whole, wsend, wrecv, hilo, ssend, srecv, keep, opposite, tsend, trecv,
    ssem, rsem, lsem,
):
    row, col = lax.axis_index("row"), lax.axis_index("col")
    z, h = row // 2, row % 2
    x, t, j = col // 4, (col // 2) % 2, col % 2
    matched = h == j
    half = 256
    lo, hi = pl.ds(0, half), pl.ds(half, half)

    def zq(d):
        return (z + d + 8) % 8

    def xq(d, other):
        return 2 * ((x + d + 4) % 4) + (1 - t if other else t)

    zp, zm = (2 * zq(1) + h, col), (2 * zq(-1) + h, col)
    xp, xm = (row, (col + 4) % 16), (row, (col + 12) % 16)
    yh = (row, 4 * x + 2 * (1 - t) + j)
    yl = (2 * z + 1 - h, col)
    core = (row, 4 * x + 2 * t + 1 - j)
    diag = (2 * z + 1 - h, 4 * x + 2 * t + 1 - j)

    count = [0]
    sent = []

    def make(src, dst, who, slot=None):
        if slot is None:
            slot = count[0]
            count[0] += 1
        return pltpu.make_async_remote_copy(
            src_ref=src, dst_ref=dst, send_sem=ssem.at[slot], recv_sem=rsem.at[slot],
            device_id=who, device_id_type=MESH,
        )

    def push(src, dst, who):
        copy = make(src, dst, who)
        copy.start()
        sent.append(copy)
        return copy

    def later(src, dst, who):
        copy = make(src, dst, who)
        sent.append(copy)
        return copy

    def same(ref, who):
        return push(ref, ref, who)

    halves = ((0, 256), (256, 256))

    first = xq(0, False)
    own_g = pltpu.make_async_copy(g_ref, gbuf.at[z], lsem.at[0])
    own_l = pltpu.make_async_copy(l_ref, lbuf.at[j, first], lsem.at[1])
    r_own = pltpu.make_async_copy(r_ref, rbuf.at[z, j], lsem.at[2])
    swaps = [
        make(l_ref.at[pl.ds(*r)], lbuf.at[1 - j, first, pl.ds(*r)], diag) for r in halves
    ]

    keep_avg = pltpu.make_async_copy(avg_in, avg, lsem.at[3])
    keep_sq = pltpu.make_async_copy(sq_in, sq, lsem.at[4])
    own_g.start()
    keep_avg.start()
    keep_sq.start()

    @pl.when(matched)
    def _():
        own_l.start()
        r_own.start()

    barrier = pltpu.get_barrier_semaphore()
    for who in (zp, zm, xp, xm, yh, yl, core, diag):
        pl.semaphore_signal(barrier, inc=1, device_id=who, device_id_type=MESH)
    pl.semaphore_wait(barrier, 8)

    @pl.when(jnp.logical_not(matched))
    def _():
        for copy in swaps:
            copy.start()

    base_r = count[0]
    count[0] += 3
    r_far = make(r_ref, rbuf.at[z, j], (2 * z + 1 - h, 4 * x + 2 * t + h), base_r + j)
    r_near = make(r_ref, rbuf.at[z, j], core, base_r + 2)

    def drain():
        for copy in sent:
            copy.wait_send()
        r_far.wait_send()
        for ring in ring_rot:
            ring.far[0].wait_send()

        @pl.when(matched)
        def _():
            for ring in ring_l:
                ring.far[0].wait_send()

        @pl.when(jnp.logical_not(matched))
        def _():
            for ring in ring_l:
                for copy in ring.ring:
                    copy.wait_send()
            for copy in swaps:
                copy.wait_send()
            r_near.wait_send()

    class RingZ:
        def __init__(self, buf, cut):
            def both(k, low, high):
                return later(low, low, zp), later(high, high, zm)

            self.steps = [both(0, buf.at[z], buf.at[z])]
            for k in (1, 2, 3):
                low, high = buf.at[zq(-k)], buf.at[zq(k)]
                if k == 3:
                    low, high = cut(low, 0), cut(high, 1)
                self.steps.append(both(k, low, high))

        def start(self):
            for copy in self.steps[0]:
                copy.start()

        def step(self, k):
            for before, copy in zip(self.steps[k - 1], self.steps[k]):
                before.wait_recv()
                copy.start()

        def finish(self):
            for copy in self.steps[3]:
                copy.wait_recv()

    class RingX:
        def __init__(self, buf, top, size):
            low, high = pl.ds(top, size // 2), pl.ds(top + size // 2, size // 2)

            def to(q, rows, who):
                return later(buf.at[q, rows], buf.at[q, rows], who)

            self.y = to(xq(0, False), pl.ds(top, size), yh)
            self.lead, self.rest = {}, {}
            for other in (False, True):
                q = xq(0, other)
                self.lead[other] = to(q, low, xp), to(q, high, xm)
                self.rest[other] = to(q, high, xp), to(q, low, xm)
            self.passed = to(xq(-1, False), low, xp), to(xq(1, False), high, xm)
            down, up, far = xq(-1, True), xq(1, True), xq(2, False)
            whole_block = buf.at[far, pl.ds(top, size)]
            self.ring = (
                make(buf.at[down, low], buf.at[down, low], xp),
                make(buf.at[up, high], buf.at[up, high], xm),
            )
            self.far = (make(whole_block, whole_block, yh),)

        def across(self):
            self.y.start()

        def go(self, other):
            for copy in self.lead[other] + self.rest[other]:
                copy.start()

        def second(self):
            self.y.wait_recv()
            self.go(True)

        def forward(self):
            for before, copy in zip(self.lead[False], self.passed):
                before.wait_recv()
                copy.start()

        def forward_ring(self):
            for before, copy in zip(self.lead[True], self.ring):
                before.wait_recv()
                copy.start()

        def forward_far(self):
            for copy in self.passed:
                copy.wait_recv()
            self.far[0].start()

        def complete(self, *others):
            for other in others:
                for copy in self.rest[other]:
                    copy.wait_recv()

        def finish_far(self):
            for copy in self.lead[True] + self.rest[True] + self.far:
                copy.wait_recv()

    ring_g = RingZ(gbuf, lambda ref, k: ref.at[lo if k == 0 else hi])
    ring_r = RingZ(rbuf, lambda ref, k: ref.at[k])
    ring_l = [RingX(lbuf.at[j], *r) for r in halves]

    order = [(0, False), (-1, False), (1, False), (2, False), (0, True), (-1, True), (1, True), (2, True)]
    shared = [later(lbuf.at[j, xq(*o)], lbuf.at[j, xq(*o)], core) for o in order]

    def share(*which):
        for n in which:
            shared[n].start()

    def take(*which):
        for n in which:
            shared[n].wait_recv()

    def left(event, *which):
        for ring in ring_l:
            getattr(ring, event)(*which)

    def rotate(i, first, number):
        def body(n, carry):
            q = 2 * ((x + n // 2 + first) % 4) + n % 2
            part[i] += dot(lbuf[i, q], gbuf[q], TN)
            return carry

        lax.fori_loop(0, number, body, 0)

    def rotate_own(other):
        def body(m, carry):
            q = 2 * ((x + m) % 4) + (1 - t if other else t)
            part[h] += dot(lbuf[h, q], gbuf[q], TN)
            return carry

        lax.fori_loop(0, 4, body, 0)

    pieces = tuple((128 * n, 128) for n in range(4))
    exchange = [later(part.at[1 - h, pl.ds(*r)], part_in.at[pl.ds(*r)], yl) for r in pieces]

    def give():
        for copy in exchange:
            copy.start()

    part[...] = jnp.zeros_like(part)

    @pl.when(matched)
    def _():
        own_l.wait()
        left("go", False)
        share(0)
        own_g.wait()
        ring_g.start()
        left("forward")
        ring_g.step(1)
        left("complete", False)
        share(1, 2)
        left("across")
        r_far.start()
        ring_g.step(2)
        left("forward_far")
        share(3)
        ring_g.step(3)
        make(r_ref, rbuf.at[z, 1 - j], core, base_r + 2).wait_recv()
        r_own.wait()
        ring_r.start()
        take(0, 1, 2, 4, 5, 6)
        left("second")
        share(4)
        ring_g.finish()
        rotate(1 - h, 3, 6)
        take(3, 7)
        rotate(1 - h, 2, 2)
        give()
        rotate_own(False)
        left("finish_far")
        share(5, 6, 7)
        ring_r.step(1)
        rotate_own(True)
        ring_r.step(2)

    @pl.when(jnp.logical_not(matched))
    def _():
        own_g.wait()
        ring_g.start()
        for ring, copy in zip(ring_l, swaps):
            copy.wait_recv()
            ring.across()
            ring.go(False)
        share(0)
        ring_g.step(1)
        left("forward")
        left("second")
        share(4)
        r_far.start()
        r_near.start()
        left("complete", False)
        share(1, 2)
        ring_g.step(2)
        left("forward_ring")
        for ring in ring_l:
            for copy in ring.passed:
                copy.wait_recv()
        share(3)
        ring_g.step(3)
        left("complete", True)
        share(5, 6)
        make(r_ref, rbuf.at[z, 0], core, base_r).wait_recv()
        make(r_ref, rbuf.at[z, 1], core, base_r + 1).wait_recv()
        ring_r.start()
        for ring in ring_l:
            for copy in ring.ring:
                copy.wait_recv()
        share(7)
        ring_g.finish()
        rotate(1 - h, 0, 8)
        give()
        ring_r.step(1)
        take(0, 1, 2, 3)
        rotate_own(False)
        take(4, 5, 6, 7)
        rotate_own(True)
        ring_r.step(2)


    ring_rot = [RingX(rot, *r) for r in halves]
    for n, r in enumerate(halves):
        exchange[2 * n].wait_recv()
        exchange[2 * n + 1].wait_recv()
        rows = pl.ds(*r)
        rot[first, rows] = (part[h, rows] + part_in[rows]).astype(BF16)
        ring_rot[n].across()
        ring_rot[n].go(False)
    ring_rot[0].forward()
    ring_rot[0].second()
    ring_r.step(3)
    ring_rot[1].forward()
    ring_rot[1].second()
    ring_rot[0].forward_far()
    ring_rot[1].forward_far()
    ring_r.finish()

    keep_avg.wait()
    keep_sq.wait()
    first_fix = 1.0 - beta_first**STEP
    second_fix = 1.0 - beta_second**STEP
    give_d = []
    for n, r in enumerate(halves):
        rows = pl.ds(*r)
        proj[:, rows] = jnp.zeros((2, 256, 256), F32)

        def project(other):
            def body(m, carry):
                q = 2 * ((x + m) % 4) + (1 - t if other else t)
                for c in range(2):
                    proj[c, rows] += dot(rot[q, rows], rbuf[q, c], NN)
                return carry

            lax.fori_loop(0, 4, body, 0)

        ring_rot[n].complete(False)
        project(False)
        ring_rot[n].finish_far()
        project(True)
        push(proj.at[1 - j, rows], proj_in.at[rows], core).wait_recv()
        projected = proj[j, rows] + proj_in[rows]
        new_avg = beta_first * avg[rows] + (1.0 - beta_first) * projected
        new_sq = beta_second * sq[rows] + (1.0 - beta_second) * projected * projected
        proj_in[rows] = projected
        dbuf[h, rows] = (
            new_avg / first_fix / (jnp.sqrt(new_sq / second_fix) + epsilon)
        ).astype(BF16)
        give_d.append(same(dbuf.at[h, rows], yl))
    out_proj = pltpu.make_async_copy(proj_in, proj_out, lsem.at[3])
    out_proj.start()
    for copy in give_d:
        copy.wait_recv()

    def quarters(n):
        return (pl.ds(256 * n, 128), pl.ds(256 * n + 128, 128))

    def spread_left(q):
        whole[q] = dot(lbuf[0, q], dbuf[0], NN) + dot(lbuf[1, q], dbuf[1], NN)

    flying = {}

    def back_send(n, s, way, k):
        rows = quarters(n)[k]
        value = whole[zq(5 - s if way == 0 else s - 5), rows]
        before = flying.get((n, way, s - 1, k))
        if before is not None:
            before.wait_recv()
            value += wrecv[way, s - 2, rows].astype(F32)
        wsend[way, s - 1, rows] = value.astype(BF16)
        flying[n, way, s, k] = push(
            wsend.at[way, s - 1, rows], wrecv.at[way, s - 1, rows], (zp, zm)[way]
        )

    def back_step(n, s):
        for k in (0, 1):
            for way in (0, 1):
                if s > 2 or k == 0:
                    back_send(n, s, way, (1 - way, way)[k] if s > 2 else way)

    def back_end(n):
        rows = pl.ds(256 * n, 256)
        value = whole[z, rows]
        for way in range(2):
            for k in range(2):
                flying[n, way, 4, k].wait_recv()
        for way in range(2):
            value += wrecv[way, 3, rows].astype(F32)
        high = value.astype(BF16)
        hilo[n, j, 0] = high
        hilo[n, j, 1] = (value - high.astype(F32)).astype(BF16)
        push(hilo.at[n, j], hilo.at[n, j], core).wait_recv()

    def spread_right(n, q):
        total = dot(hilo[n, 0].reshape(512, 256), rbuf[q, 0], NT)
        total += dot(hilo[n, 1].reshape(512, 256), rbuf[q, 1], NT)
        return total[:256] + total[256:]

    going, last = {}, {}

    def send(key, slot, n, k, value):
        rows = pl.ds(256 * n, 256) if k is None else quarters(n)[k]
        ssend[slot, rows] = value.astype(BF16)
        going[key] = push(
            ssend.at[slot, rows], srecv.at[slot, rows], yh if slot == 0 else (xp, xm)[slot % 2 == 0]
        )

    def part_of(value, k):
        return value[128 * k : 128 * k + 128]

    def up_first(n):
        send((n, 0), 0, n, None, spread_right(n, xq(2, True)))
        for way in range(2):
            send((n, 1 + way), 1 + way, n, None, spread_right(n, xq(1 - 2 * way, True)))
        for way in range(2):
            value = spread_right(n, xq(1 - 2 * way, False))
            send((n, 3 + way, 1 - way), 3 + way, n, 1 - way, part_of(value, 1 - way))
            keep[way, quarters(n)[way]] = part_of(value, way)
        opposite[n] = spread_right(n, xq(2, False))

    def up_second(n):
        going[n, 0].wait_recv()
        for way in range(2):
            rows = quarters(n)[way]
            value = opposite[n, 128 * way : 128 * way + 128] + srecv[0, rows].astype(F32)
            send((n, 5 + way), 5 + way, n, way, value)

    def up_third(n):
        rows = pl.ds(256 * n, 256)
        value = spread_right(n, xq(0, True))
        for way in range(2):
            going[n, 1 + way].wait_recv()
            value += srecv[1 + way, rows].astype(F32)
        tsend[rows] = value.astype(BF16)
        last[n] = push(tsend.at[rows], trecv.at[rows], yh)

    def up_fourth(n):
        for way in range(2):
            rows = quarters(n)[way]
            going[n, 5 + way].wait_recv()
            send((n, 3 + way, way), 3 + way, n, way, keep[way, rows] + srecv[5 + way, rows].astype(F32))

    def up_last(n):
        rows = pl.ds(256 * n, 256)
        value = spread_right(n, xq(0, False))
        for way in range(2):
            for k in range(2):
                going[n, 3 + way, k].wait_recv()
            value += srecv[3 + way, rows].astype(F32)
        update[rows] = value

    def back_open(s):
        for n in range(2):
            for way in range(2):
                back_send(n, s, way, way if s == 1 else 1 - way)

    spread_left(zq(4))
    back_open(1)
    spread_left(zq(3))
    spread_left(zq(-3))
    back_open(2)
    spread_left(zq(2))
    spread_left(zq(-2))
    back_step(0, 2)
    back_step(1, 2)
    spread_left(zq(1))
    spread_left(zq(-1))
    back_step(0, 3)
    back_step(1, 3)
    spread_left(z)
    back_step(0, 4)
    back_step(1, 4)
    back_end(0)
    up_first(0)
    back_end(1)
    up_first(1)
    up_second(0)
    up_third(0)
    up_second(1)
    up_fourth(0)
    up_third(1)
    up_last(0)
    up_fourth(1)
    up_last(1)
    out_near = pltpu.make_async_copy(update, near_out, lsem.at[4])
    out_near.start()
    for n in range(2):
        last[n].wait_recv()
    out_far = pltpu.make_async_copy(trecv, far_out, lsem.at[5])
    out_far.start()
    drain()
    out_proj.wait()
    out_near.wait()
    out_far.wait()


def shards(grad, left_basis, right_basis, exp_avg, exp_avg_sq):
    block = jax.ShapeDtypeStruct((512, 256), F32)
    place = pl.BlockSpec(memory_space=pl.ANY)
    near, far, projected = pl.pallas_call(
        kernel,
        out_shape=(block, jax.ShapeDtypeStruct((512, 256), BF16), block),
        in_specs=[place] * 5,
        out_specs=(place,) * 3,
        scratch_shapes=[
            pltpu.VMEM((512, 256), F32),
            pltpu.VMEM((512, 256), F32),
            pltpu.VMEM((512, 256), F32),
            pltpu.VMEM((8, 512, 256), BF16),
            pltpu.VMEM((2, 8, 512, 512), BF16),
            pltpu.VMEM((8, 2, 256, 256), BF16),
            pltpu.VMEM((8, 512, 256), BF16),
            pltpu.VMEM((2, 512, 256), F32),
            pltpu.VMEM((512, 256), F32),
            pltpu.VMEM((2, 512, 256), F32),
            pltpu.VMEM((512, 256), F32),
            pltpu.VMEM((2, 512, 256), BF16),
            pltpu.VMEM((8, 512, 256), F32),
            pltpu.VMEM((2, 4, 512, 256), BF16),
            pltpu.VMEM((2, 4, 512, 256), BF16),
            pltpu.VMEM((2, 2, 2, 256, 256), BF16),
            pltpu.VMEM((7, 512, 256), BF16),
            pltpu.VMEM((7, 512, 256), BF16),
            pltpu.VMEM((2, 512, 256), F32),
            pltpu.VMEM((2, 256, 256), F32),
            pltpu.VMEM((512, 256), BF16),
            pltpu.VMEM((512, 256), BF16),
            pltpu.SemaphoreType.DMA((COPIES,)),
            pltpu.SemaphoreType.DMA((COPIES,)),
            pltpu.SemaphoreType.DMA((6,)),
        ],
        compiler_params=pltpu.CompilerParams(
            collective_id=0, has_side_effects=True, vmem_limit_bytes=56 * 1024 * 1024
        ),
        cost_estimate=pl.CostEstimate(flops=6_500_000_000, bytes_accessed=4_000_000, transcendentals=0),
    )(grad, left_basis, right_basis, exp_avg, exp_avg_sq)
    new_avg = beta_first * exp_avg + (1.0 - beta_first) * projected
    new_sq = beta_second * exp_avg_sq + (1.0 - beta_second) * projected * projected
    return near + far.astype(F32), new_avg, new_sq


def solution(mesh):
    return jax.shard_map(
        shards,
        mesh=mesh,
        in_specs=(
            P("row", "col"),
            P("col", "row"),
            P("row", "col"),
            P("row", "col"),
            P("row", "col"),
        ),
        out_specs=(P("row", "col"), P("row", "col"), P("row", "col")),
        check_vma=False,
    )
```
